128 devices in a mesh: ctx: 8 (over y, core), head: 16 (over z, x).
Axes of the slice: x: 4, y: 4, z: 4, core: 2. Of those that a mesh axis runs over, the one named last changes fastest.
Arguments:
- tokens: bfloat16 [8192, 2048], P('ctx', 'head'), may hold values from -6 to 6
- beta: float32 [8192, 16], P('ctx', 'head'), may hold values from 0 to 2
- w_query: bfloat16 [2048, 2048], P(None, 'head'), may hold values from -0.125 to 0.125
- w_key: bfloat16 [2048, 2048], P(None, 'head'), may hold values from -0.125 to 0.125
- w_value: bfloat16 [2048, 2048], P(None, 'head'), may hold values from -0.125 to 0.125
- gain: float32 [128], replicated, may hold values from 0.25 to 1.75
- w_out: bfloat16 [2048, 2048], P('head'), may hold values from -0.125 to 0.125
Outputs:
- mixed: bfloat16 [8192, 2048], P(('ctx', 'head'))
The draws below stay inside these ranges and needn't reach their ends.
All inputs are finite; a program needn't handle non-finite values.
Results may differ from the reference program's by a relative error of at most 0.023.
Values may be sent and summed in bfloat16 or wider, within the bound.
No kernel may reach another device: no remote copies, remote signals or barrier semaphores. Data moves between devices by JAX's collectives and lax.ppermute only.
A program may use at most 64 MiB of HBM per device.

```python
import jax
import jax.numpy as jnp
from jax import lax

D = 2048
DK = 128
BLOCK = 64
H = 16
SLAB_TOKENS = 8192


def draw_beta(key, part):
    key = jax.random.fold_in(key, 11)
    gradual_key, quick_key, selection_key, jitter_key, spike_key = jax.random.split(key, 5)
    slow_rate = DK * jax.random.uniform(gradual_key, (H,), jnp.float32, 0.2, 1.0) / SLAB_TOKENS
    fast_rate = jax.random.uniform(quick_key, (H,), jnp.float32, 0.3, 0.8)
    ranking = jax.random.permutation(selection_key, H)
    fast_count = H // 2
    baseline_rate = jnp.where(ranking < fast_count, fast_rate, slow_rate)
    jitter_level = jax.random.uniform(jitter_key, (SLAB_TOKENS, H), jnp.float32, 0.5, 1.5)
    locations = jax.random.randint(spike_key, (8,), 0, SLAB_TOKENS)
    positions = jnp.arange(SLAB_TOKENS, dtype=jnp.int32)[:, None]
    spike_level = jnp.any(positions == locations[None, :], axis=1)
    value_rows = jnp.where(spike_level[:, None], 1.5, baseline_rate[None, :] * jitter_level)
    return value_rows.astype(jnp.float32)


def levels(rng, extent, cuts, smallest, high):
    level, own = 1.0, jax.random.fold_in(rng, 6)
    for dim, blocks in cuts:
        heights = jnp.exp(jax.random.uniform(jax.random.fold_in(own, dim), (blocks,), jnp.float32, smallest / len(cuts), high / len(cuts)))
        level = level * jnp.repeat(heights, extent[dim] // blocks).reshape([-1 if axis == dim else 1 for axis in range(len(extent))])
    return level


def centred(rng, dims, deviation, limit, cuts=(), kind=jnp.bfloat16):
    result = jax.random.normal(rng, dims, jnp.float32) * deviation
    if len(cuts) > 0:
        result = levels(rng, dims, cuts, -0.22, 0.18) * result
    return jnp.clip(result, min=-limit, max=limit).astype(kind)


def setup_inputs(seed: int = 0) -> dict:
    arg_keys = jax.random.split(jax.random.key(seed), 8)
    return {
        "tokens": centred(arg_keys[0], (SLAB_TOKENS, D), 1.0, 6.0, ((0, 8), (1, 16))),
        "beta": draw_beta(jax.random.fold_in(arg_keys[7], 71), 0),
        "w_query": centred(arg_keys[2], (D, H * DK), D ** -0.5, 0.125, ((1, 16),)),
        "w_key": centred(arg_keys[3], (D, H * DK), D ** -0.5, 0.125, ((1, 16),)),
        "w_value": centred(arg_keys[4], (D, H * DK), D ** -0.5, 0.125, ((1, 16),)),
        "gain": jnp.clip(1.0 + 0.15 * jax.random.normal(arg_keys[5], (DK,), jnp.float32), 0.25, 1.75),
        "w_out": centred(arg_keys[6], (H * DK, D), (H * DK) ** -0.5, 0.125, ((0, 16),)),
    }


def matmul(left, right):
    return jnp.dot(left.astype(jnp.float32), right.astype(jnp.float32), precision=lax.Precision.HIGHEST, preferred_element_type=jnp.float32)

def unit_rows(matrix):
    return matrix * lax.rsqrt(lax.optimization_barrier(jnp.sum(matrix * matrix, axis=-1, keepdims=True)) + 1e-06)

def head_run(operands):
    queries, keys, value_rows, rates = operands
    count = queries.shape[0] // BLOCK
    blocked = (queries.reshape(count, BLOCK, DK), keys.reshape(count, BLOCK, DK), value_rows.reshape(count, BLOCK, DK), rates.reshape(count, BLOCK))

    def advance(memory_state, block_data):
        block_query, block_key, block_value, block_rate = block_data
        lower_tri = jnp.tril(block_rate[:, None] * matmul(block_key, block_key.T), -1) + jnp.eye(BLOCK, dtype=jnp.float32)
        key_factor = jax.scipy.linalg.solve_triangular(lower_tri, block_rate[:, None] * block_key, lower=True, unit_diagonal=True)
        value_factor = jax.scipy.linalg.solve_triangular(lower_tri, block_rate[:, None] * block_value, lower=True, unit_diagonal=True)
        written = value_factor - matmul(key_factor, memory_state.T)
        output_rows = matmul(block_query, memory_state.T) + matmul(jnp.tril(matmul(block_query, block_key.T)), written)
        memory_state = memory_state + matmul(written.T, block_key)
        return (memory_state, output_rows)
    _, outputs = lax.scan(advance, jnp.zeros((DK, DK), jnp.float32), blocked)
    return outputs.reshape(count * BLOCK, DK)

def reference(tokens, beta, w_query, w_key, w_value, gain, w_out):

    def project(weight):
        raw_proj = jnp.dot(tokens.astype(jnp.float32), weight.astype(jnp.float32), preferred_element_type=jnp.float32)
        return raw_proj.reshape(SLAB_TOKENS, H, DK).transpose(1, 0, 2)
    queries = unit_rows(jax.nn.silu(project(w_query)))
    keys = unit_rows(jax.nn.silu(project(w_key)))
    value_rows = project(w_value)
    recurrent = lax.map(head_run, (queries, keys, value_rows, beta.T))
    scale_inv = lax.rsqrt(lax.optimization_barrier(jnp.mean(recurrent * recurrent, axis=-1, keepdims=True)) + 1e-05)
    normed = (recurrent * scale_inv * gain).astype(jnp.bfloat16)
    normed = normed.transpose(1, 0, 2).reshape(SLAB_TOKENS, H * DK)
    return jnp.dot(normed.astype(jnp.float32), w_out.astype(jnp.float32), preferred_element_type=jnp.float32).astype(jnp.bfloat16)
```

```python
import jax
import jax.numpy as jnp
from jax import lax
from jax.experimental import pallas as pl
from jax.experimental.pallas import tpu as pltpu
from jax.sharding import PartitionSpec as P

DK = 128
CHUNK = 128
F32 = jnp.float32
BF16 = jnp.bfloat16
SMEM = pl.BlockSpec(memory_space=pltpu.SMEM)
VMEM = pl.BlockSpec(memory_space=pltpu.VMEM)
LIMIT = 40 << 20


def dot(left, right, contract=((1,), (0,))):
    return lax.dot_general(
        left.astype(BF16), right.astype(BF16), (contract, ((), ())), preferred_element_type=F32
    )


def swap(value, even, odd, ctx, heads):
    pairs = [
        (c * heads + h, c * heads + (h ^ (odd if c % 2 else even)))
        for c in range(ctx)
        for h in range(heads)
    ]
    return lax.ppermute(value, ("ctx", "head"), pairs)


ALONG_X = ((1, 3), (3, 1))
ALONG_Z = ((4, 12), (12, 4))


def doubled(value, masks, ctx, heads):
    return swap(value, *masks, ctx, heads)


def piece_heads(first, second):
    me = lax.axis_index("head")
    core = lax.axis_index("ctx") % 2

    def of_core(c):
        orders = []
        for axis in (first, second):
            one, two = axis[0][c], axis[1][c]
            orders.append([0, one, two, one ^ two])
        return jnp.array([b ^ a for b in orders[1] for a in orders[0]], jnp.int32)

    own = me ^ jnp.where(core == 0, of_core(0), of_core(1))
    other = me ^ jnp.where(core == 0, of_core(1), of_core(0))
    return own, other


def project_part(heads_ref, pieces_ref, weights, base):
    total = None
    for p in range(0, 8, 2):
        left = jnp.concatenate([pieces_ref[p], pieces_ref[p + 1]], axis=1)
        rows = []
        for q in (p, p + 1):
            start = pl.multiple_of(heads_ref[base + q] * DK, DK)
            rows.append(
                jnp.concatenate([w[pl.ds(start, DK), :] for w in weights], axis=1)
            )
        term = jnp.dot(left, jnp.concatenate(rows, axis=0), preferred_element_type=F32)
        total = term if total is None else total + term
    return total


def first_half_kernel(ha, hb, a_ref, b_ref, wq, wk, wv, raw_ref):
    half = a_ref.shape[1]
    raw_ref[:half, :] = project_part(ha, a_ref, (wq, wk, wv), 0)
    raw_ref[half:, :] = project_part(hb, b_ref, (wq, wk, wv), 0)


def unit_silu(raw):
    act = raw / (1.0 + jnp.exp(jnp.minimum(-raw, 80.0)))
    return act * lax.rsqrt(jnp.sum(act * act, axis=-1, keepdims=True) + 1e-6)


def transition_kernel(
    ha, hb, raw_ref, a_ref, b_ref, wq, wk, wv, beta_ref,
    q_ref, k_ref, wu_ref, states_ref, last_ref, total_ref,
):
    rows = raw_ref.shape[0]
    half = rows // 2
    count = rows // CHUNK
    total_ref[:half, :] = raw_ref[:half, :] + project_part(ha, a_ref, (wq, wk, wv), 8)
    total_ref[half:, :] = raw_ref[half:, :] + project_part(hb, b_ref, (wq, wk, wv), 8)
    row = lax.broadcasted_iota(jnp.int32, (CHUNK, CHUNK), 0)
    col = lax.broadcasted_iota(jnp.int32, (CHUNK, CHUNK), 1)
    eye = (row == col).astype(F32)

    def below(size):
        return (row // (2 * size) == col // (2 * size)) & (
            (row // size) % 2 == 1
        ) & ((col // size) % 2 == 0)

    keys, rates, lowers, inverses = [], [], [], []
    for b in range(count):
        part = slice(b * CHUNK, (b + 1) * CHUNK)
        q_ref[part, :] = unit_silu(total_ref[part, :DK]).astype(BF16)
        key = unit_silu(total_ref[part, DK : 2 * DK])
        key16 = key.astype(BF16)
        k_ref[part, :] = key16
        rate = jnp.transpose(jnp.broadcast_to(beta_ref[b : b + 1, :], (CHUNK, CHUNK)))
        gram = dot(key16, key16, ((1,), (1,)))
        lower = jnp.where(row > col, rate * gram, 0.0)
        keys.append(key)
        rates.append(rate)
        lowers.append(lower)
        inverses.append(eye - jnp.where(below(1), lower, 0.0))
    size = 2
    while size < CHUNK:
        mask = below(size)
        inner = [dot(jnp.where(mask, lo, 0.0), inv) for lo, inv in zip(lowers, inverses)]
        inverses = [inv - dot(inv, x) for inv, x in zip(inverses, inner)]
        size *= 2
    maps = []
    for b in range(count):
        part = slice(b * CHUNK, (b + 1) * CHUNK)
        value = total_ref[part, 2 * DK :]
        both = jnp.concatenate([rates[b] * keys[b], rates[b] * value], axis=1)
        wu = dot(inverses[b], both).astype(BF16)
        wu_ref[part, :] = wu
        maps.append(dot(k_ref[part, :], wu, ((0,), (0,))))
    zeros = jnp.zeros((DK, DK), F32)
    state = jnp.concatenate([eye, zeros], axis=1)
    for b in range(count):
        state16 = state.astype(BF16)
        states_ref[b] = state16
        state = (
            state
            - dot(maps[b][:, :DK], state16)
            + jnp.concatenate([zeros, maps[b][:, DK:]], axis=1)
        )
    last_ref[...] = state


def outputs_kernel(q_ref, k_ref, wu_ref, states_ref, query_ref, out_ref):
    rows = q_ref.shape[0]
    row = lax.broadcasted_iota(jnp.int32, (CHUNK, CHUNK), 0)
    col = lax.broadcasted_iota(jnp.int32, (CHUNK, CHUNK), 1)
    for b in range(rows // CHUNK):
        part = slice(b * CHUNK, (b + 1) * CHUNK)
        query = q_ref[part, :]
        scores = jnp.where(row >= col, dot(query, k_ref[part, :], ((1,), (1,))), 0.0)
        local = dot(scores, wu_ref[part, :])
        effective = query.astype(F32) - local[:, :DK]
        result = dot(effective, states_ref[b])
        query_ref[part, :] = result[:, :DK].astype(BF16)
        out_ref[part, :] = result[:, DK:] + local[:, DK:]


def compose(later, earlier):
    return dot(later[:, :DK], earlier) + jnp.concatenate(
        [jnp.zeros((DK, DK), F32), later[:, DK:]], axis=1
    )


def merge_kernel(upper_ref, span_ref, prefix_ref, other_ref, new_span_ref, new_prefix_ref):
    span, prefix = span_ref[...], prefix_ref[...]
    other = other_ref[...].astype(F32)
    upper = upper_ref[0] == 1
    later = jnp.where(upper, span, other)
    earlier = jnp.where(upper, other, span)
    new_span_ref[...] = compose(later, earlier)
    new_prefix_ref[...] = jnp.where(upper, compose(prefix, other), prefix)


def finish_kernel(upper_ref, prefix_ref, other_ref, query_ref, out_ref, gain_ref, normed_ref):
    prefix = prefix_ref[...]
    other = other_ref[...].astype(F32)
    entering = jnp.where(
        upper_ref[0] == 1,
        dot(prefix[:, :DK], other[:, DK:]) + prefix[:, DK:],
        prefix[:, DK:],
    )
    recurrent = out_ref[...] + dot(query_ref[...], entering)
    scale = lax.rsqrt(jnp.mean(recurrent * recurrent, axis=-1, keepdims=True) + 1e-5)
    normed_ref[...] = (recurrent * scale * gain_ref[...]).astype(BF16)


def mix_kernel(h0, h1, h2, h3, x_ref, *refs):
    pieces, mixed_ref, total_ref = refs[:8], refs[8], refs[9]
    step = pl.program_id(0)
    heads = (h0, h1, h2, h3)
    width = total_ref.shape[1] // 4

    @pl.when(step == 0)
    def _():
        total_ref[...] = jnp.zeros_like(total_ref)

    for quarter in range(4):
        term = None
        for late in range(2):
            piece = pieces[2 * quarter + late]
            j = 8 * late + 2 * step
            left = jnp.concatenate(
                [x_ref[heads[quarter][j]], x_ref[heads[quarter][j + 1]]], axis=1
            )
            right = jnp.concatenate([piece[0], piece[1]], axis=0)
            part = jnp.dot(left, right, preferred_element_type=F32)
            term = part if term is None else term + part
        total_ref[:, quarter * width : (quarter + 1) * width] += term

    @pl.when(step == pl.num_programs(0) - 1)
    def _():
        mixed_ref[...] = total_ref[...].astype(BF16)


def call(kernel, shapes, n_smem, n_vmem, scratch=(), flops=0, size=0):
    return pl.pallas_call(
        kernel,
        out_shape=shapes,
        in_specs=[SMEM] * n_smem + [VMEM] * n_vmem,
        out_specs=jax.tree.map(lambda _: VMEM, shapes),
        scratch_shapes=list(scratch),
        compiler_params=pltpu.CompilerParams(vmem_limit_bytes=LIMIT),
        cost_estimate=pl.CostEstimate(flops=flops, bytes_accessed=size, transcendentals=0),
    )


def struct(shape, dtype):
    return jax.ShapeDtypeStruct(shape, dtype)


def local(tokens, beta, w_query, w_key, w_value, gain, w_out):
    ctx, heads = lax.axis_size("ctx"), lax.axis_size("head")
    rows = tokens.shape[0]
    half = rows // 2
    me_ctx = lax.axis_index("ctx")
    weights = (w_query, w_key, w_value)
    ha, other_a = piece_heads(ALONG_X, ALONG_Z)
    hb, other_b = piece_heads(ALONG_Z, ALONG_X)

    def spread(a, b):
        a, b = a[None], b[None]
        for step in range(4):
            am = (ALONG_X + ALONG_Z)[step]
            bm = (ALONG_Z + ALONG_X)[step]
            na, nb = swap(a, *am, ctx, heads), swap(b, *bm, ctx, heads)
            if step < 3:
                a = jnp.concatenate([a, na], axis=0)
                b = jnp.concatenate([b, nb], axis=0)
        return a, b, na, nb

    ta, tb, na, nb = spread(tokens[:half], tokens[half:])
    raw = call(
        first_half_kernel, struct((rows, 3 * DK), F32), 2, 5, flops=rows * 1024 * 768, size=5 << 20
    )(ha, hb, ta, tb, *weights)
    query, key, wu, states, last = call(
        transition_kernel,
        (
            struct((rows, DK), BF16),
            struct((rows, DK), BF16),
            struct((rows, 2 * DK), BF16),
            struct((rows // CHUNK, DK, 2 * DK), BF16),
            struct((DK, 2 * DK), F32),
        ),
        2, 7,
        scratch=[pltpu.VMEM((rows, 3 * DK), F32)],
        flops=rows * 4096 * 768, size=8 << 20,
    )(ha, hb, raw, na, nb, *weights, beta.reshape(rows // CHUNK, CHUNK))

    core = me_ctx % 2
    width = w_out.shape[1] // 4
    mine = lax.dynamic_slice_in_dim(w_out, core * 2 * width, 2 * width, axis=1)
    oa, ob, pa, pb = spread(mine[:, :width], mine[:, width:])
    flip = [(c, c ^ 1) for c in range(ctx)]
    theirs = [lax.ppermute(v, "ctx", flip) for v in (oa, pa, ob, pb)]
    ours = [oa, pa, ob, pb]

    eff_query, partial = call(
        outputs_kernel,
        (struct((rows, DK), BF16), struct((rows, DK), F32)),
        0, 4,
        flops=rows * 2048 * 256, size=4 << 20,
    )(query, key, wu, states)

    span = last
    prefix = jnp.concatenate([jnp.eye(DK, dtype=F32), jnp.zeros((DK, DK), F32)], axis=1)
    bits = (1, 2)
    for bit in bits:
        other = lax.ppermute(span.astype(BF16), "ctx", [(c, c ^ bit) for c in range(ctx)])
        upper = ((me_ctx // bit) % 2).astype(jnp.int32)[None]
        span, prefix = call(
            merge_kernel, (struct((DK, 2 * DK), F32),) * 2, 1, 3, flops=1 << 24, size=1 << 19
        )(upper, span, prefix, other)
    other = lax.ppermute(span.astype(BF16), "ctx", [(c, c ^ 6) for c in range(ctx)])
    upper = (me_ctx // 4).astype(jnp.int32)[None]
    normed = call(
        finish_kernel, struct((rows, DK), BF16), 1, 5, flops=rows * 128 * 256, size=2 << 20
    )(upper, prefix, other, eff_query, partial, gain[None, :])

    spread_rows = lax.all_to_all(normed, "head", 0, 0, tiled=True).reshape(
        heads, rows // heads, DK
    )

    def mix(blocks_lo, heads_lo, blocks_hi, heads_hi):
        piece = pl.BlockSpec((2, DK, width), lambda i: (i, 0, 0))
        return pl.pallas_call(
            mix_kernel,
            grid=(4,),
            out_shape=struct((rows // heads, 4 * width), BF16),
            in_specs=[SMEM] * 4
            + [pl.BlockSpec((heads, rows // heads, DK), lambda i: (0, 0, 0))]
            + [piece] * 8,
            out_specs=pl.BlockSpec((rows // heads, 4 * width), lambda i: (0, 0)),
            scratch_shapes=[pltpu.VMEM((rows // heads, 4 * width), F32)],
            compiler_params=pltpu.CompilerParams(vmem_limit_bytes=LIMIT),
            cost_estimate=pl.CostEstimate(
                flops=64 * 2048 * 4096, bytes_accessed=9 << 20, transcendentals=0
            ),
        )(*heads_lo, *heads_hi, spread_rows, *blocks_lo, *blocks_hi)

    return lax.cond(
        core == 0,
        lambda: mix(ours, (ha, hb), theirs, (other_a, other_b)),
        lambda: mix(theirs, (other_a, other_b), ours, (ha, hb)),
    )


def solution(mesh):
    placed = (
        P("ctx", "head"),
        P("ctx", "head"),
        P(None, "head"),
        P(None, "head"),
        P(None, "head"),
        P(),
        P("head", None),
    )
    return jax.shard_map(
        local, mesh=mesh, in_specs=placed, out_specs=P(("ctx", "head"), None), check_vma=False
    )
```

```python
import jax
import jax.numpy as jnp
from jax import lax
from jax.experimental import pallas as pl
from jax.experimental.pallas import tpu as pltpu
from jax.sharding import PartitionSpec as P

DK = 128
CHUNK = 128
F32 = jnp.float32
BF16 = jnp.bfloat16
VMEM = pl.BlockSpec(memory_space=pltpu.VMEM)
LIMIT = 14 << 20


def dot(left, right, contract=((1,), (0,))):
    return lax.dot_general(
        left.astype(BF16), right.astype(BF16), (contract, ((), ())), preferred_element_type=F32
    )


ALONG_X = ((1, 3), (3, 1))
ALONG_Z = ((4, 12), (12, 4))


OPPOSITE = (12, 4)


def flipped(masks):
    return tuple((odd, even) for even, odd in masks)


STREAMS = (
    ALONG_X + ALONG_Z,
    ALONG_Z + ALONG_X,
    flipped(ALONG_X + ALONG_Z),
    flipped(ALONG_Z + ALONG_X),
)


def swap(value, masks, ctx, heads):
    pairs = [
        (c * heads + h, c * heads + (h ^ masks[c % 2])) for c in range(ctx) for h in range(heads)
    ]
    return lax.ppermute(value, ("ctx", "head"), pairs)


def offsets(masks, core):
    order = [0]
    for step in masks:
        order = order + [o ^ step[core] for o in order]
    return order


class Place:
    def __init__(self):
        ctx, head = lax.axis_index("ctx"), lax.axis_index("head")
        self.core, self.y = lax.rem(ctx, 2), lax.div(ctx, 2)
        self.head, self.z, self.x = head, lax.div(head, 4), lax.rem(head, 4)
        self.first_core = self.core == 0

    def by_core(self, first, second):
        return jnp.where(self.first_core, first, second)

    def piece_heads(self, masks):
        return [self.head ^ self.by_core(a, b) for a, b in zip(offsets(masks, 0), offsets(masks, 1))]


def pack_kernel(tokens_ref, w_ref, p0, p1, p2, p3, sems):
    place = Place()
    quarter = place.core * 2 + lax.rem(place.y, 2)
    copies = []
    for stream, out in enumerate((p0, p1, p2, p3)):
        for i in range(2):
            start = (2 * stream + i) * DK
            copies.append(
                (tokens_ref.at[start : start + DK, :], out.at[0, :, i * DK : (i + 1) * DK])
            )
    for i in range(2):
        start = pl.multiple_of(quarter * 512 + i * 256, 256)
        copies.append((w_ref.at[:, pl.ds(start, 256)], p0.at[1 + i]))
    started = []
    for n, (source, target) in enumerate(copies):
        copy = pltpu.make_async_copy(source, target, sems.at[n])
        copy.start()
        started.append(copy)
    for copy in started:
        copy.wait()


def join_kernel(*refs):
    out_ref, at = refs[-1], 0
    for ref in refs[:-1]:
        out_ref[at : at + ref.shape[0]] = ref[...]
        at += ref.shape[0]


def split_kernel(one_ref, two_ref, tokens_ref, w_ref):
    for i in range(4):
        source, at = (one_ref, two_ref)[i // 2], 3 * (i % 2)
        tokens_ref[i] = source[at]
        w_ref[2 * i] = source[at + 1]
        w_ref[2 * i + 1] = source[at + 2]


def project_part(heads, pieces_ref, weights):
    total = None
    for p in range(0, 8, 2):
        left = jnp.concatenate(
            [
                jnp.concatenate(
                    [pieces_ref[q, :, i * DK : (i + 1) * DK] for q in (p, p + 1)], axis=1
                )
                for i in range(2)
            ],
            axis=0,
        )
        rows = []
        for q in (p, p + 1):
            start = pl.multiple_of(heads[q] * DK, DK)
            rows.append(jnp.concatenate([w[pl.ds(start, DK), :] for w in weights], axis=1))
        term = jnp.dot(left, jnp.concatenate(rows, axis=0), preferred_element_type=F32)
        total = term if total is None else total + term
    return total


def first_half_kernel(t0, t1, t2, t3, wq, wk, wv, raw_ref):
    place = Place()
    for i, pieces in enumerate((t0, t1, t2, t3)):
        heads = place.piece_heads(STREAMS[i])[:8]
        raw_ref[i * 256 : (i + 1) * 256, :] = project_part(heads, pieces, (wq, wk, wv))


def unit_silu(raw):
    act = raw / (1.0 + jnp.exp(jnp.minimum(-raw, 80.0)))
    return act * lax.rsqrt(jnp.sum(act * act, axis=-1, keepdims=True) + 1e-6)


def transition_kernel(
    raw_ref, t0, t1, t2, t3, wq, wk, wv, beta_ref,
    q_ref, k_ref, wu_ref, states_ref, last_ref, sent_ref, total_ref,
):
    rows = raw_ref.shape[0]
    count = rows // CHUNK
    place = Place()
    for i, pieces in enumerate((t0, t1, t2, t3)):
        part = slice(i * 256, (i + 1) * 256)
        heads = place.piece_heads(STREAMS[i])[8:]
        total_ref[part, :] = raw_ref[part, :] + project_part(heads, pieces, (wq, wk, wv))
    row = lax.broadcasted_iota(jnp.int32, (CHUNK, CHUNK), 0)
    col = lax.broadcasted_iota(jnp.int32, (CHUNK, CHUNK), 1)
    eye = (row == col).astype(F32)

    def below(size):
        return (row // (2 * size) == col // (2 * size)) & (
            (row // size) % 2 == 1
        ) & ((col // size) % 2 == 0)

    keys, rates, lowers, inverses = [], [], [], []
    for b in range(count):
        part = slice(b * CHUNK, (b + 1) * CHUNK)
        q_ref[part, :] = unit_silu(total_ref[part, :DK]).astype(BF16)
        key = unit_silu(total_ref[part, DK : 2 * DK])
        key16 = key.astype(BF16)
        k_ref[part, :] = key16
        rate = jnp.transpose(jnp.broadcast_to(beta_ref[b : b + 1, :], (CHUNK, CHUNK)))
        gram = dot(key16, key16, ((1,), (1,)))
        lower = jnp.where(row > col, rate * gram, 0.0)
        keys.append(key)
        rates.append(rate)
        lowers.append(lower)
        inverses.append(eye - jnp.where(below(1), lower, 0.0))
    size = 2
    while size < CHUNK:
        mask = below(size)
        inner = [dot(jnp.where(mask, lo, 0.0), inv) for lo, inv in zip(lowers, inverses)]
        inverses = [inv - dot(inv, x) for inv, x in zip(inverses, inner)]
        size *= 2
    maps = []
    for b in range(count):
        part = slice(b * CHUNK, (b + 1) * CHUNK)
        value = total_ref[part, 2 * DK :]
        both = jnp.concatenate([rates[b] * keys[b], rates[b] * value], axis=1)
        wu = dot(inverses[b], both).astype(BF16)
        wu_ref[part, :] = wu
        maps.append(dot(k_ref[part, :], wu, ((0,), (0,))))
    zeros = jnp.zeros((DK, DK), F32)
    state = jnp.concatenate([eye, zeros], axis=1)
    for b in range(count):
        state16 = state.astype(BF16)
        states_ref[b] = state16
        state = (
            state
            - dot(maps[b][:, :DK], state16)
            + jnp.concatenate([zeros, maps[b][:, DK:]], axis=1)
        )
    last_ref[...] = state
    sent_ref[...] = state.astype(BF16)


def outputs_kernel(q_ref, k_ref, wu_ref, states_ref, query_ref, out_ref):
    rows = q_ref.shape[0]
    row = lax.broadcasted_iota(jnp.int32, (CHUNK, CHUNK), 0)
    col = lax.broadcasted_iota(jnp.int32, (CHUNK, CHUNK), 1)
    for b in range(rows // CHUNK):
        part = slice(b * CHUNK, (b + 1) * CHUNK)
        query = q_ref[part, :]
        scores = jnp.where(row >= col, dot(query, k_ref[part, :], ((1,), (1,))), 0.0)
        local = dot(scores, wu_ref[part, :])
        effective = query.astype(F32) - local[:, :DK]
        result = dot(effective, states_ref[b])
        query_ref[part, :] = result[:, :DK].astype(BF16)
        out_ref[part, :] = result[:, DK:] + local[:, DK:]


def compose(later, earlier):
    return dot(later[:, :DK], earlier) + jnp.concatenate(
        [jnp.zeros((DK, DK), F32), later[:, DK:]], axis=1
    )


def chip_kernel(mine_ref, other_ref, chip_ref):
    mine, other = mine_ref[...], other_ref[...].astype(F32)
    second = Place().core == 1
    chip_ref[...] = compose(
        jnp.where(second, mine, other), jnp.where(second, other, mine)
    ).astype(BF16)


def finish_kernel(
    third_ref, second_ref, first_ref, other_ref, query_ref, out_ref, gain_ref, normed_ref
):
    place = Place()
    entering = third_ref[:, DK:].astype(F32)
    for earlier in (second_ref, first_ref):
        entering = dot(earlier[:, :DK], entering) + earlier[:, DK:].astype(F32)
    after_other = dot(other_ref[:, :DK], entering) + other_ref[:, DK:].astype(F32)
    entering = jnp.where(place.core == 1, after_other, entering)
    recurrent = out_ref[...] + dot(query_ref[...], entering)
    scale = lax.rsqrt(jnp.mean(recurrent * recurrent, axis=-1, keepdims=True) + 1e-5)
    normed = (recurrent * scale * gain_ref[...]).astype(BF16)
    for b in range(16):
        z, x = b // 4, b % 4
        inside = place.by_core(
            lax.div(place.z, 2) == z // 2, (place.z == z) | (place.z == 3 - z)
        )
        seat = place.by_core(jnp.where(inside, z % 2, 1 - z % 2), z // 2)
        slot = (seat * 4 + x) * 2 + jnp.where(inside, 0, 1)
        start = pl.multiple_of(slot * 64, 64)
        normed_ref[pl.ds(start, 64), :] = normed[b * 64 : (b + 1) * 64, :]


def mix_rows(x_ref, near_ref, far_ref, rows, out_ref, dtype):
    place = Place()
    seat = place.by_core(lax.rem(place.z, 2), lax.div(place.z, 2))
    along_x = [offsets(STREAMS[0][:2], core) for core in range(2)]
    even = lax.rem(place.y, 2)
    for side in range(2):
        core = place.core if side == 0 else 1 - place.core
        order = [
            place.x ^ place.by_core(along_x[side][j], along_x[1 - side][j]) for j in range(4)
        ]
        lefts = {}
        for group in range(2):
            base = (seat if group == 0 else 1 - seat) * 4
            for j in (0, 2):
                lefts[group, j] = jnp.concatenate(
                    [x_ref[base + order[j], rows, :], x_ref[base + order[j + 1], rows, :]], axis=1
                )
        for quarter in range(2):
            column = (core * 2 + (even if quarter == 0 else 1 - even)) * 512
            for slab in range(2):
                total = None
                for group, ref in enumerate((near_ref, far_ref)):
                    at = side * 16 + quarter * 8 + slab
                    for j in (0, 2):
                        right = jnp.concatenate([ref[at + 2 * j], ref[at + 2 * j + 2]], axis=0)
                        term = jnp.dot(lefts[group, j], right, preferred_element_type=F32)
                        total = term if total is None else total + term
                start = pl.multiple_of(column + slab * 256, 256)
                out_ref[:, pl.ds(start, 256)] = total.astype(dtype)


def mix_partner_kernel(x_ref, near_ref, far_ref, out_ref):
    mix_rows(x_ref, near_ref, far_ref, slice(64, 128), out_ref, BF16)


def mix_own_kernel(x_ref, near_ref, far_ref, out_ref):
    mix_rows(x_ref, near_ref, far_ref, slice(0, 64), out_ref, F32)


def sum_kernel(own_ref, other_ref, mixed_ref):
    mixed_ref[...] = (own_ref[...] + other_ref[...].astype(F32)).astype(BF16)


def call(kernel, shapes, n_vmem, scratch=(), flops=0, size=0):
    return pl.pallas_call(
        kernel,
        out_shape=shapes,
        in_specs=[VMEM] * n_vmem,
        out_specs=jax.tree.map(lambda _: VMEM, shapes),
        scratch_shapes=list(scratch),
        compiler_params=pltpu.CompilerParams(vmem_limit_bytes=LIMIT),
        cost_estimate=pl.CostEstimate(flops=flops, bytes_accessed=size, transcendentals=0),
    )


def struct(shape, dtype):
    return jax.ShapeDtypeStruct(shape, dtype)


def join(*parts):
    shape = (sum(p.shape[0] for p in parts),) + parts[0].shape[1:]
    return call(join_kernel, struct(shape, BF16), len(parts), size=1 << 20)(*parts)


def local(tokens, beta, w_query, w_key, w_value, gain, w_out):
    ctx, heads = lax.axis_size("ctx"), lax.axis_size("head")
    rows = tokens.shape[0]
    weights = (w_query, w_key, w_value)

    slab = (DK, 2 * DK)
    pieces = pl.pallas_call(
        pack_kernel,
        out_shape=tuple(struct((n,) + slab, BF16) for n in (3, 1, 1, 1)),
        in_specs=[pl.BlockSpec(memory_space=pltpu.HBM)] * 2,
        out_specs=(VMEM,) * 4,
        scratch_shapes=[pltpu.SemaphoreType.DMA((10,))],
        compiler_params=pltpu.CompilerParams(vmem_limit_bytes=LIMIT),
    )(tokens, w_out)
    arrived = [swap(p, masks[0], ctx, heads) for p, masks in zip(pieces, STREAMS)]
    arrived = lax.optimization_barrier(arrived)
    pieces = [join(p, n) for p, n in zip(pieces, arrived)]
    arrived = [swap(p, masks[1], ctx, heads) for p, masks in zip(pieces, STREAMS)]
    arrived = lax.optimization_barrier(arrived)
    first, w = call(
        split_kernel, (struct((4,) + slab, BF16), struct((8,) + slab, BF16)), 2, size=2 << 20
    )(pieces[0], arrived[0])
    pieces = [first] + [join(p, n) for p, n in zip(pieces[1:], arrived[1:])]
    w_next = lax.ppermute(w, "ctx", [(c, c ^ 2) for c in range(ctx)])
    arrived = [swap(p, masks[2], ctx, heads) for p, masks in zip(pieces, STREAMS)]
    *arrived, w_next = lax.optimization_barrier((*arrived, w_next))
    w = join(w, w_next)
    other_core = [(c, c ^ 1) for c in range(ctx)]
    pieces = [join(p, n) for p, n in zip(pieces, arrived)]
    arrived = [swap(p, masks[3], ctx, heads) for p, masks in zip(pieces, STREAMS)]
    raw = call(
        first_half_kernel, struct((rows, 3 * DK), F32), 7, flops=rows * 1024 * 768, size=5 << 20
    )(*pieces, *weights)
    w_next = lax.ppermute(w, "ctx", other_core)
    *arrived, w_next, raw = lax.optimization_barrier((*arrived, w_next, raw))
    near = join(w, w_next)
    far = swap(near, (4, 12), ctx, heads)

    query, key, wu, states, last, sent = call(
        transition_kernel,
        (
            struct((rows, DK), BF16),
            struct((rows, DK), BF16),
            struct((rows, 2 * DK), BF16),
            struct((rows // CHUNK, DK, 2 * DK), BF16),
            struct((DK, 2 * DK), F32),
            struct((DK, 2 * DK), BF16),
        ),
        9,
        scratch=[pltpu.VMEM((rows, 3 * DK), F32)],
        flops=rows * 4096 * 768, size=8 << 20,
    )(raw, *arrived, *weights, beta.reshape(rows // CHUNK, CHUNK))
    eff_query, partial = call(
        outputs_kernel,
        (struct((rows, DK), BF16), struct((rows, DK), F32)),
        4,
        flops=rows * 2048 * 256, size=4 << 20,
    )(query, key, wu, states)

    other = lax.ppermute(sent, "ctx", other_core)
    other, eff_query, partial = lax.optimization_barrier((other, eff_query, partial))
    chip = call(
        chip_kernel, struct((DK, 2 * DK), BF16), 2, flops=1 << 23, size=1 << 18
    )(last, other)
    one, two, three = [
        lax.ppermute(chip, "ctx", [(c, c + 2 * k) for c in range(ctx - 2 * k)])
        for k in (1, 2, 3)
    ]

    normed = call(
        finish_kernel, struct((rows, DK), BF16), 7, flops=rows * 128 * 256, size=2 << 20
    )(three, two, one, other, eff_query, partial, gain[None, :])
    pairs = (((0, 1), (2, 3)), ((0, 3), (1, 2)))
    groups = [
        [c * heads + z * 4 + x for z in pair for x in range(4)]
        for c in range(ctx)
        for pair in pairs[c % 2]
    ]
    spread_rows = lax.all_to_all(
        normed, ("ctx", "head"), 0, 0, tiled=True, axis_index_groups=groups
    ).reshape(8, 2 * rows // heads, DK)

    operands = (spread_rows, near, far)
    leaving = call(
        mix_partner_kernel, struct((64, 2048), BF16), 3, flops=64 * 2048 * 2048, size=4 << 20
    )(*operands)
    entering = swap(leaving, OPPOSITE, ctx, heads)
    own = call(
        mix_own_kernel, struct((64, 2048), F32), 3, flops=64 * 2048 * 2048, size=4 << 20
    )(*operands)
    return call(sum_kernel, struct((64, 2048), BF16), 2, size=1 << 20)(own, entering)


def solution(mesh):
    placed = (
        P("ctx", "head"),
        P("ctx", "head"),
        P(None, "head"),
        P(None, "head"),
        P(None, "head"),
        P(),
        P("head", None),
    )
    return jax.shard_map(
        local, mesh=mesh, in_specs=placed, out_specs=P(("ctx", "head"), None), check_vma=False
    )
```

```python
import jax
import jax.numpy as jnp
from jax import lax
from jax.experimental import pallas as pl
from jax.experimental.pallas import tpu as pltpu
from jax.sharding import PartitionSpec as P

DK = 128
CHUNK = 128
F32 = jnp.float32
BF16 = jnp.bfloat16
VMEM = pl.BlockSpec(memory_space=pltpu.VMEM)
LIMIT = 14 << 20


def dot(left, right, contract=((1,), (0,))):
    return lax.dot_general(
        left.astype(BF16), right.astype(BF16), (contract, ((), ())), preferred_element_type=F32
    )


ALONG_X = ((1, 3), (3, 1))
ALONG_Z = ((4, 12), (12, 4))


OPPOSITE = (12, 4)


def flipped(masks):
    return tuple((odd, even) for even, odd in masks)


OPPOSITE = (12, 4)


def flipped(masks):
    return tuple((odd, even) for even, odd in masks)


STREAMS = (
    ALONG_X + ALONG_Z,
    ALONG_Z + ALONG_X,
    flipped(ALONG_X + ALONG_Z),
    flipped(ALONG_Z + ALONG_X),
)


STREAMS = (
    ALONG_X + ALONG_Z,
    ALONG_Z + ALONG_X,
    ALONG_X + flipped(ALONG_Z),
    ALONG_Z + flipped(ALONG_X),
)


def swap(value, masks, ctx, heads):
    pairs = [
        (c * heads + h, c * heads + (h ^ masks[c % 2])) for c in range(ctx) for h in range(heads)
    ]
    return lax.ppermute(value, ("ctx", "head"), pairs)


def offsets(masks, core):
    order = [0]
    for step in masks:
        order = order + [o ^ step[core] for o in order]
    return order


class Place:
    def __init__(self):
        ctx, head = lax.axis_index("ctx"), lax.axis_index("head")
        self.core, self.y = lax.rem(ctx, 2), lax.div(ctx, 2)
        self.head, self.z, self.x = head, lax.div(head, 4), lax.rem(head, 4)
        self.first_core = self.core == 0

    def by_core(self, first, second):
        return jnp.where(self.first_core, first, second)

    def piece_heads(self, masks):
        return [self.head ^ self.by_core(a, b) for a, b in zip(offsets(masks, 0), offsets(masks, 1))]


def pack_kernel(tokens_ref, a_ref, b_ref):
    for stream, out in enumerate((a_ref, b_ref)):
        for i in range(4):
            start = (2 * stream + i % 2 + 4 * (i // 2)) * DK
            at = (i % 2) * DK
            out[i // 2, :, at : at + DK] = tokens_ref[start : start + DK, :]


def pack_with_w_kernel(piece_ref, w_ref, out_ref):
    place = Place()
    quarter = place.core * 2 + lax.rem(place.y, 2)
    out_ref[:2] = piece_ref[...]
    for k in range(2):
        start = pl.multiple_of(quarter * 512 + k * 256, 256)
        out_ref[2 + k] = w_ref[:, pl.ds(start, 256)]


def join_kernel(*refs):
    out_ref, at = refs[-1], 0
    for ref in refs[:-1]:
        out_ref[at : at + ref.shape[0]] = ref[...]
        at += ref.shape[0]


def split_kernel(one_ref, two_ref, first_ref, second_ref, *w_ref):
    width = one_ref.shape[0] // 2
    for i in range(4):
        source, at = (one_ref, two_ref)[i // 2], width * (i % 2)
        first_ref[i] = source[at]
        second_ref[i] = source[at + 1]
        if w_ref:
            w_ref[0][2 * i : 2 * i + 2] = source[at + 2 : at + 4]


def project_part(heads, pieces_ref, weights):
    total = None
    for p in range(0, 8, 2):
        left = jnp.concatenate(
            [
                jnp.concatenate(
                    [pieces_ref[q, :, i * DK : (i + 1) * DK] for q in (p, p + 1)], axis=1
                )
                for i in range(2)
            ],
            axis=0,
        )
        rows = []
        for q in (p, p + 1):
            start = pl.multiple_of(heads[q] * DK, DK)
            rows.append(jnp.concatenate([w[pl.ds(start, DK), :] for w in weights], axis=1))
        term = jnp.dot(left, jnp.concatenate(rows, axis=0), preferred_element_type=F32)
        total = term if total is None else total + term
    return total


def first_half_kernel(t0, t1, t2, t3, wq, wk, wv, raw_ref):
    place = Place()
    for i, pieces in enumerate((t0, t1, t2, t3)):
        heads = place.piece_heads(STREAMS[i])[:8]
        raw_ref[i * 256 : (i + 1) * 256, :] = project_part(heads, pieces, (wq, wk, wv))


def unit_silu(raw):
    act = raw / (1.0 + jnp.exp(jnp.minimum(-raw, 80.0)))
    return act * lax.rsqrt(jnp.sum(act * act, axis=-1, keepdims=True) + 1e-6)


def transition_kernel(
    raw_ref, t0, t1, t2, t3, wq, wk, wv, beta_ref,
    q_ref, k_ref, wu_ref, states_ref, last_ref, sent_ref, total_ref,
):
    rows = raw_ref.shape[0]
    count = rows // CHUNK
    place = Place()
    for i, pieces in enumerate((t0, t1, t2, t3)):
        part = slice(i * 256, (i + 1) * 256)
        heads = place.piece_heads(STREAMS[i])[8:]
        total_ref[part, :] = raw_ref[part, :] + project_part(heads, pieces, (wq, wk, wv))
    row = lax.broadcasted_iota(jnp.int32, (CHUNK, CHUNK), 0)
    col = lax.broadcasted_iota(jnp.int32, (CHUNK, CHUNK), 1)
    eye = (row == col).astype(F32)

    def below(size):
        return (row // (2 * size) == col // (2 * size)) & (
            (row // size) % 2 == 1
        ) & ((col // size) % 2 == 0)

    keys, rates, lowers, inverses = [], [], [], []
    for b in range(count):
        part = slice(b * CHUNK, (b + 1) * CHUNK)
        q_ref[part, :] = unit_silu(total_ref[part, :DK]).astype(BF16)
        key = unit_silu(total_ref[part, DK : 2 * DK])
        key16 = key.astype(BF16)
        k_ref[part, :] = key16
        rate = jnp.transpose(jnp.broadcast_to(beta_ref[b : b + 1, :], (CHUNK, CHUNK)))
        gram = dot(key16, key16, ((1,), (1,)))
        lower = jnp.where(row > col, rate * gram, 0.0)
        keys.append(key)
        rates.append(rate)
        lowers.append(lower)
        inverses.append(eye - jnp.where(below(1), lower, 0.0))
    size = 2
    while size < CHUNK:
        mask = below(size)
        inner = [dot(jnp.where(mask, lo, 0.0), inv) for lo, inv in zip(lowers, inverses)]
        inverses = [inv - dot(inv, x) for inv, x in zip(inverses, inner)]
        size *= 2
    maps = []
    for b in range(count):
        part = slice(b * CHUNK, (b + 1) * CHUNK)
        value = total_ref[part, 2 * DK :]
        both = jnp.concatenate([rates[b] * keys[b], rates[b] * value], axis=1)
        wu = dot(inverses[b], both).astype(BF16)
        wu_ref[part, :] = wu
        maps.append(dot(k_ref[part, :], wu, ((0,), (0,))))
    zeros = jnp.zeros((DK, DK), F32)
    state = jnp.concatenate([eye, zeros], axis=1)
    for b in range(count):
        state16 = state.astype(BF16)
        states_ref[b] = state16
        state = (
            state
            - dot(maps[b][:, :DK], state16)
            + jnp.concatenate([zeros, maps[b][:, DK:]], axis=1)
        )
    last_ref[...] = state
    sent_ref[...] = state.astype(BF16)


def outputs_kernel(q_ref, k_ref, wu_ref, states_ref, query_ref, out_ref):
    rows = q_ref.shape[0]
    row = lax.broadcasted_iota(jnp.int32, (CHUNK, CHUNK), 0)
    col = lax.broadcasted_iota(jnp.int32, (CHUNK, CHUNK), 1)
    for b in range(rows // CHUNK):
        part = slice(b * CHUNK, (b + 1) * CHUNK)
        query = q_ref[part, :]
        scores = jnp.where(row >= col, dot(query, k_ref[part, :], ((1,), (1,))), 0.0)
        local = dot(scores, wu_ref[part, :])
        effective = query.astype(F32) - local[:, :DK]
        result = dot(effective, states_ref[b])
        query_ref[part, :] = result[:, :DK].astype(BF16)
        out_ref[part, :] = result[:, DK:] + local[:, DK:]


def compose(later, earlier):
    return dot(later[:, :DK], earlier) + jnp.concatenate(
        [jnp.zeros((DK, DK), F32), later[:, DK:]], axis=1
    )


def apply(step, state):
    return dot(step[:, :DK], state) + step[:, DK:]


def chip_kernel(mine_ref, other_ref, chip_ref):
    mine, other = mine_ref[...], other_ref[...].astype(F32)
    second = Place().core == 1
    chip_ref[...] = compose(
        jnp.where(second, mine, other), jnp.where(second, other, mine)
    ).astype(BF16)


def pair_kernel(mine_ref, other_ref, sent_ref):
    mine, other = mine_ref[...].astype(F32), other_ref[...].astype(F32)
    odd = lax.rem(Place().y, 2) == 1
    sent_ref[...] = apply(jnp.where(odd, mine, other), jnp.where(odd, other, mine)[:, DK:]).astype(
        BF16
    )


def finish_kernel(pair_ref, chip_ref, core_ref, query_ref, out_ref, gain_ref, normed_ref):
    place = Place()
    entering = jnp.where(place.y >= 2, pair_ref[...].astype(F32), 0.0)
    entering = jnp.where(
        lax.rem(place.y, 2) == 1, apply(chip_ref[...].astype(F32), entering), entering
    )
    entering = jnp.where(place.core == 1, apply(core_ref[...].astype(F32), entering), entering)
    recurrent = out_ref[...] + dot(query_ref[...], entering)
    scale = lax.rsqrt(jnp.mean(recurrent * recurrent, axis=-1, keepdims=True) + 1e-5)
    normed = (recurrent * scale * gain_ref[...]).astype(BF16)
    for b in range(16):
        z, x = b // 4, b % 4
        inside = place.by_core(
            lax.div(place.z, 2) == z // 2, (place.z == z) | (place.z == 3 - z)
        )
        seat = place.by_core(jnp.where(inside, z % 2, 1 - z % 2), z // 2)
        slot = (seat * 4 + x) * 2 + jnp.where(inside, 0, 1)
        start = pl.multiple_of(slot * 64, 64)
        normed_ref[pl.ds(start, 64), :] = normed[b * 64 : (b + 1) * 64, :]


def mix_rows(x_ref, refs, rows, out_ref, dtype):
    place = Place()
    seat = place.by_core(lax.rem(place.z, 2), lax.div(place.z, 2))
    along_x = [offsets(ALONG_X, c) for c in range(2)]
    even = lax.rem(place.y, 2)
    for side in range(2):
        core = place.core if side == 0 else 1 - place.core
        order = [
            place.x ^ place.by_core(along_x[side][j], along_x[1 - side][j]) for j in range(4)
        ]
        lefts = {}
        for group in range(2):
            base = (seat if group == 0 else 1 - seat) * 4
            for j in (0, 2):
                lefts[group, j] = jnp.concatenate(
                    [x_ref[base + order[j], rows, :], x_ref[base + order[j + 1], rows, :]], axis=1
                )
        for slab in range(4):
            total = None
            for group, ref in enumerate((refs[side], refs[2 + side])):
                for j in (0, 2):
                    at = (slab // 2) * 8 + j * 2 + slab % 2
                    right = jnp.concatenate([ref[at], ref[at + 2]], axis=0)
                    term = jnp.dot(lefts[group, j], right, preferred_element_type=F32)
                    total = term if total is None else total + term
            parity = even if slab < 2 else 1 - even
            start = pl.multiple_of((core * 2 + parity) * 512 + (slab % 2) * 256, 256)
            out_ref[:, pl.ds(start, 256)] = total.astype(dtype)


def mix_partner_kernel(x_ref, *refs):
    mix_rows(x_ref, refs[:4], slice(64, 128), refs[4], BF16)


def mix_own_kernel(x_ref, *refs):
    mix_rows(x_ref, refs[:4], slice(0, 64), refs[4], F32)


def sum_kernel(own_ref, other_ref, mixed_ref):
    mixed_ref[...] = (own_ref[...] + other_ref[...].astype(F32)).astype(BF16)


def call(kernel, shapes, n_vmem, scratch=(), flops=0, size=0):
    return pl.pallas_call(
        kernel,
        out_shape=shapes,
        in_specs=[VMEM] * n_vmem,
        out_specs=jax.tree.map(lambda _: VMEM, shapes),
        scratch_shapes=list(scratch),
        compiler_params=pltpu.CompilerParams(vmem_limit_bytes=LIMIT),
        cost_estimate=pl.CostEstimate(flops=flops, bytes_accessed=size, transcendentals=0),
    )


def struct(shape, dtype):
    return jax.ShapeDtypeStruct(shape, dtype)


def join(*parts):
    shape = (sum(p.shape[0] for p in parts),) + parts[0].shape[1:]
    return call(join_kernel, struct(shape, BF16), len(parts), size=1 << 20)(*parts)


def local(tokens, beta, w_query, w_key, w_value, gain, w_out):
    ctx, heads = lax.axis_size("ctx"), lax.axis_size("head")
    rows = tokens.shape[0]
    weights = (w_query, w_key, w_value)

    slab = (DK, 2 * DK)
    a, b = call(pack_kernel, (struct((2,) + slab, BF16),) * 2, 1, size=1 << 19)(tokens)
    a = call(pack_with_w_kernel, struct((4,) + slab, BF16), 2, size=1 << 20)(a, w_out)
    na, nb = swap(a, STREAMS[0][0], ctx, heads), swap(b, STREAMS[1][0], ctx, heads)
    na, nb = lax.optimization_barrier((na, nb))
    a, b = join(a, na), join(b, nb)
    na, nb = swap(a, STREAMS[0][1], ctx, heads), swap(b, STREAMS[1][1], ctx, heads)
    four = struct((4,) + slab, BF16)
    pieces = [None] * 4
    pieces[0], pieces[2], w = call(
        split_kernel, (four, four, struct((8,) + slab, BF16)), 2, size=2 << 20
    )(a, na)
    pieces[1], pieces[3] = call(split_kernel, (four, four), 2, size=1 << 20)(b, nb)
    *_, w = lax.optimization_barrier((*pieces, w))
    other_core = [(c, c ^ 1) for c in range(ctx)]
    w_next = lax.ppermute(w, "ctx", [(c, c ^ 2) for c in range(ctx)])
    arrived = [swap(p, masks[2], ctx, heads) for p, masks in zip(pieces, STREAMS)]
    pieces = [join(p, n) for p, n in zip(pieces, arrived)]
    arrived = [swap(p, masks[3], ctx, heads) for p, masks in zip(pieces, STREAMS)]
    raw = call(
        first_half_kernel, struct((rows, 3 * DK), F32), 7, flops=rows * 1024 * 768, size=5 << 20
    )(*pieces, *weights)
    *arrived, w_next, raw = lax.optimization_barrier((*arrived, w_next, raw))
    w = join(w, w_next)
    far_a = swap(w, (4, 12), ctx, heads)
    w_next = lax.ppermute(w, "ctx", other_core)

    query, key, wu, states, last, sent = call(
        transition_kernel,
        (
            struct((rows, DK), BF16),
            struct((rows, DK), BF16),
            struct((rows, 2 * DK), BF16),
            struct((rows // CHUNK, DK, 2 * DK), BF16),
            struct((DK, 2 * DK), F32),
            struct((DK, 2 * DK), BF16),
        ),
        9,
        scratch=[pltpu.VMEM((rows, 3 * DK), F32)],
        flops=rows * 4096 * 768, size=8 << 20,
    )(raw, *arrived, *weights, beta.reshape(rows // CHUNK, CHUNK))
    eff_query, partial = call(
        outputs_kernel,
        (struct((rows, DK), BF16), struct((rows, DK), F32)),
        4,
        flops=rows * 2048 * 256, size=4 << 20,
    )(query, key, wu, states)

    _, w_next = lax.optimization_barrier((sent, w_next))
    far_b = swap(w_next, (4, 12), ctx, heads)
    of_core = lax.ppermute(sent, "ctx", other_core)
    chip = call(
        chip_kernel, struct((DK, 2 * DK), BF16), 2, flops=1 << 23, size=1 << 18
    )(last, of_core)
    of_chip = lax.ppermute(chip, "ctx", [(c, c ^ 2) for c in range(ctx)])
    of_chip, eff_query, partial = lax.optimization_barrier((of_chip, eff_query, partial))
    pair = call(pair_kernel, struct((DK, DK), BF16), 2, flops=1 << 23, size=1 << 18)(chip, of_chip)
    of_pair = lax.ppermute(pair, "ctx", [(c, c ^ 6) for c in range(ctx)])
    normed = call(
        finish_kernel, struct((rows, DK), BF16), 6, flops=rows * 128 * 256, size=2 << 20
    )(of_pair, of_chip, of_core, eff_query, partial, gain[None, :])
    pairs = (((0, 1), (2, 3)), ((0, 3), (1, 2)))
    groups = [
        [c * heads + z * 4 + x for z in pair for x in range(4)]
        for c in range(ctx)
        for pair in pairs[c % 2]
    ]
    spread_rows = lax.all_to_all(
        normed, ("ctx", "head"), 0, 0, tiled=True, axis_index_groups=groups
    ).reshape(8, 2 * rows // heads, DK)

    operands = (spread_rows, w, w_next, far_a, far_b)
    leaving = call(
        mix_partner_kernel, struct((64, 2048), BF16), 5, flops=64 * 2048 * 2048, size=4 << 20
    )(*operands)
    entering = swap(leaving, OPPOSITE, ctx, heads)
    own = call(
        mix_own_kernel, struct((64, 2048), F32), 5, flops=64 * 2048 * 2048, size=4 << 20
    )(*operands)
    return call(sum_kernel, struct((64, 2048), BF16), 2, size=1 << 20)(own, entering)


def solution(mesh):
    placed = (
        P("ctx", "head"),
        P("ctx", "head"),
        P(None, "head"),
        P(None, "head"),
        P(None, "head"),
        P(),
        P("head", None),
    )
    return jax.shard_map(
        local, mesh=mesh, in_specs=placed, out_specs=P(("ctx", "head"), None), check_vma=False
    )
```

```python
import jax
import jax.numpy as jnp
from jax import lax
from jax.experimental import pallas as pl
from jax.experimental.pallas import tpu as pltpu
from jax.sharding import PartitionSpec as P

DK = 128
CHUNK = 128
F32 = jnp.float32
BF16 = jnp.bfloat16
VMEM = pl.BlockSpec(memory_space=pltpu.VMEM)
LIMIT = 14 << 20


def dot(left, right, contract=((1,), (0,))):
    return lax.dot_general(
        left.astype(BF16), right.astype(BF16), (contract, ((), ())), preferred_element_type=F32
    )


ALONG_X = ((1, 3), (3, 1))
ALONG_Z = ((4, 12), (12, 4))


OPPOSITE = (12, 4)


def flipped(masks):
    return tuple((odd, even) for even, odd in masks)


OPPOSITE = (12, 4)


def flipped(masks):
    return tuple((odd, even) for even, odd in masks)


STREAMS = (
    ALONG_X + ALONG_Z,
    ALONG_Z + ALONG_X,
    flipped(ALONG_X + ALONG_Z),
    flipped(ALONG_Z + ALONG_X),
)


STREAMS = (
    ALONG_X + ALONG_Z,
    ALONG_Z + ALONG_X,
    ALONG_X + flipped(ALONG_Z),
    ALONG_Z + flipped(ALONG_X),
)


def swap(value, masks, ctx, heads):
    pairs = [
        (c * heads + h, c * heads + (h ^ masks[c % 2])) for c in range(ctx) for h in range(heads)
    ]
    return lax.ppermute(value, ("ctx", "head"), pairs)


def offsets(masks, core):
    order = [0]
    for step in masks:
        order = order + [o ^ step[core] for o in order]
    return order


class Place:
    def __init__(self):
        ctx, head = lax.axis_index("ctx"), lax.axis_index("head")
        self.core, self.y = lax.rem(ctx, 2), lax.div(ctx, 2)
        self.head, self.z, self.x = head, lax.div(head, 4), lax.rem(head, 4)
        self.first_core = self.core == 0

    def by_core(self, first, second):
        return jnp.where(self.first_core, first, second)

    def piece_heads(self, masks):
        return [self.head ^ self.by_core(a, b) for a, b in zip(offsets(masks, 0), offsets(masks, 1))]


def pack_kernel(tokens_ref, a_ref, b_ref):
    for stream, out in enumerate((a_ref, b_ref)):
        for i in range(4):
            start = (2 * stream + i % 2 + 4 * (i // 2)) * DK
            at = (i % 2) * DK
            out[i // 2, :, at : at + DK] = tokens_ref[start : start + DK, :]


def pack_with_w_kernel(piece_ref, w_ref, out_ref):
    place = Place()
    quarter = place.core * 2 + lax.rem(place.y, 2)
    out_ref[:2] = piece_ref[...]
    for k in range(2):
        start = pl.multiple_of(quarter * 512 + k * 256, 256)
        out_ref[2 + k] = w_ref[:, pl.ds(start, 256)]


def join_kernel(*refs):
    out_ref, at = refs[-1], 0
    for ref in refs[:-1]:
        out_ref[at : at + ref.shape[0]] = ref[...]
        at += ref.shape[0]


def split_kernel(one_ref, two_ref, first_ref, second_ref, *w_ref):
    width = one_ref.shape[0] // 2
    for i in range(4):
        source, at = (one_ref, two_ref)[i // 2], width * (i % 2)
        first_ref[i] = source[at]
        second_ref[i] = source[at + 1]
        if w_ref:
            w_ref[0][2 * i : 2 * i + 2] = source[at + 2 : at + 4]


def project_part(heads, pieces_ref, weights):
    total = None
    for p in range(0, 8, 2):
        left = jnp.concatenate(
            [
                jnp.concatenate(
                    [pieces_ref[q, :, i * DK : (i + 1) * DK] for q in (p, p + 1)], axis=1
                )
                for i in range(2)
            ],
            axis=0,
        )
        rows = []
        for q in (p, p + 1):
            start = pl.multiple_of(heads[q] * DK, DK)
            rows.append(jnp.concatenate([w[pl.ds(start, DK), :] for w in weights], axis=1))
        term = jnp.dot(left, jnp.concatenate(rows, axis=0), preferred_element_type=F32)
        total = term if total is None else total + term
    return total


def first_half_kernel(t0, t1, t2, t3, wq, wk, wv, raw_ref):
    place = Place()
    for i, pieces in enumerate((t0, t1, t2, t3)):
        heads = place.piece_heads(STREAMS[i])[:8]
        raw_ref[i * 256 : (i + 1) * 256, :] = project_part(heads, pieces, (wq, wk, wv))


def unit_silu(raw):
    act = raw / (1.0 + jnp.exp(jnp.minimum(-raw, 80.0)))
    return act * lax.rsqrt(jnp.sum(act * act, axis=-1, keepdims=True) + 1e-6)


def transition_kernel(
    raw_ref, t0, t1, t2, t3, wk, wv, beta_ref,
    k_ref, wu_ref, states_ref, last_ref, sent_ref, total_ref,
):
    rows = raw_ref.shape[0]
    count = rows // CHUNK
    place = Place()
    for i, pieces in enumerate((t0, t1, t2, t3)):
        part = slice(i * 256, (i + 1) * 256)
        heads = place.piece_heads(STREAMS[i])[8:]
        total_ref[part, :] = raw_ref[part, DK:] + project_part(heads, pieces, (wk, wv))
    row = lax.broadcasted_iota(jnp.int32, (CHUNK, CHUNK), 0)
    col = lax.broadcasted_iota(jnp.int32, (CHUNK, CHUNK), 1)
    eye = (row == col).astype(F32)

    def below(size):
        return (row // (2 * size) == col // (2 * size)) & (
            (row // size) % 2 == 1
        ) & ((col // size) % 2 == 0)

    keys, rates, lowers, inverses = [], [], [], []
    for b in range(count):
        part = slice(b * CHUNK, (b + 1) * CHUNK)
        key = unit_silu(total_ref[part, :DK])
        key16 = key.astype(BF16)
        k_ref[part, :] = key16
        rate = jnp.transpose(jnp.broadcast_to(beta_ref[b : b + 1, :], (CHUNK, CHUNK)))
        gram = dot(key16, key16, ((1,), (1,)))
        lower = jnp.where(row > col, rate * gram, 0.0)
        keys.append(key)
        rates.append(rate)
        lowers.append(lower)
        inverses.append(eye - jnp.where(below(1), lower, 0.0))
    size = 2
    while size < CHUNK:
        mask = below(size)
        inner = [dot(jnp.where(mask, lo, 0.0), inv) for lo, inv in zip(lowers, inverses)]
        inverses = [inv - dot(inv, x) for inv, x in zip(inverses, inner)]
        size *= 2
    maps = []
    for b in range(count):
        part = slice(b * CHUNK, (b + 1) * CHUNK)
        value = total_ref[part, DK:]
        both = jnp.concatenate([rates[b] * keys[b], rates[b] * value], axis=1)
        wu = dot(inverses[b], both).astype(BF16)
        wu_ref[part, :] = wu
        maps.append(dot(k_ref[part, :], wu, ((0,), (0,))))
    zeros = jnp.zeros((DK, DK), F32)
    half = count // 2
    states = [jnp.concatenate([eye, zeros], axis=1)] * 2
    for b in range(half):
        for side in range(2):
            chunk = side * half + b
            state16 = states[side].astype(BF16)
            states_ref[chunk] = states[side]
            states[side] = (
                states[side]
                - dot(maps[chunk][:, :DK], state16)
                + jnp.concatenate([zeros, maps[chunk][:, DK:]], axis=1)
            )
    states_ref[count] = states[0]
    last = compose(states[1], states[0])
    last_ref[...] = last
    sent_ref[...] = last.astype(BF16)


def outputs_kernel(
    raw_ref, t0, t1, t2, t3, wq, k_ref, wu_ref, states_ref, query_ref, out_ref, total_ref
):
    rows = raw_ref.shape[0]
    count = rows // CHUNK
    place = Place()
    for i, pieces in enumerate((t0, t1, t2, t3)):
        part = slice(i * 256, (i + 1) * 256)
        heads = place.piece_heads(STREAMS[i])[8:]
        total_ref[part, :] = raw_ref[part, :DK] + project_part(heads, pieces, (wq,))
    row = lax.broadcasted_iota(jnp.int32, (CHUNK, CHUNK), 0)
    col = lax.broadcasted_iota(jnp.int32, (CHUNK, CHUNK), 1)
    for b in range(count):
        part = slice(b * CHUNK, (b + 1) * CHUNK)
        query = unit_silu(total_ref[part, :])
        scores = jnp.where(row >= col, dot(query, k_ref[part, :], ((1,), (1,))), 0.0)
        local = dot(scores, wu_ref[part, :])
        effective = query - local[:, :DK]
        state = states_ref[b]
        if b >= count // 2:
            state = compose(state, states_ref[count])
        result = dot(effective, state)
        query_ref[part, :] = result[:, :DK].astype(BF16)
        out_ref[part, :] = result[:, DK:] + local[:, DK:]


def compose(later, earlier):
    return dot(later[:, :DK], earlier) + jnp.concatenate(
        [jnp.zeros((DK, DK), F32), later[:, DK:]], axis=1
    )


def apply(step, state):
    return dot(step[:, :DK], state) + step[:, DK:]


def chip_kernel(mine_ref, other_ref, chip_ref):
    mine, other = mine_ref[...], other_ref[...].astype(F32)
    second = Place().core == 1
    chip_ref[...] = compose(
        jnp.where(second, mine, other), jnp.where(second, other, mine)
    ).astype(BF16)


def pair_kernel(mine_ref, other_ref, sent_ref):
    mine, other = mine_ref[...].astype(F32), other_ref[...].astype(F32)
    odd = lax.rem(Place().y, 2) == 1
    sent_ref[...] = apply(jnp.where(odd, mine, other), jnp.where(odd, other, mine)[:, DK:]).astype(
        BF16
    )


def finish_kernel(pair_ref, chip_ref, core_ref, query_ref, out_ref, gain_ref, normed_ref):
    place = Place()
    entering = jnp.where(place.y >= 2, pair_ref[...].astype(F32), 0.0)
    entering = jnp.where(
        lax.rem(place.y, 2) == 1, apply(chip_ref[...].astype(F32), entering), entering
    )
    entering = jnp.where(place.core == 1, apply(core_ref[...].astype(F32), entering), entering)
    recurrent = out_ref[...] + dot(query_ref[...], entering)
    scale = lax.rsqrt(jnp.mean(recurrent * recurrent, axis=-1, keepdims=True) + 1e-5)
    normed = (recurrent * scale * gain_ref[...]).astype(BF16)
    for b in range(16):
        z, x = b // 4, b % 4
        inside = place.by_core(
            lax.div(place.z, 2) == z // 2, (place.z == z) | (place.z == 3 - z)
        )
        seat = place.by_core(jnp.where(inside, z % 2, 1 - z % 2), z // 2)
        slot = (seat * 4 + x) * 2 + jnp.where(inside, 0, 1)
        start = pl.multiple_of(slot * 64, 64)
        normed_ref[pl.ds(start, 64), :] = normed[b * 64 : (b + 1) * 64, :]


def mix_rows(x_ref, refs, rows, out_ref, dtype):
    place = Place()
    seat = place.by_core(lax.rem(place.z, 2), lax.div(place.z, 2))
    along_x = [offsets(ALONG_X, c) for c in range(2)]
    even = lax.rem(place.y, 2)
    for side in range(2):
        core = place.core if side == 0 else 1 - place.core
        order = [
            place.x ^ place.by_core(along_x[side][j], along_x[1 - side][j]) for j in range(4)
        ]
        lefts = {}
        for group in range(2):
            base = (seat if group == 0 else 1 - seat) * 4
            for j in (0, 2):
                lefts[group, j] = jnp.concatenate(
                    [x_ref[base + order[j], rows, :], x_ref[base + order[j + 1], rows, :]], axis=1
                )
        for slab in range(4):
            total = None
            for group, ref in enumerate((refs[side], refs[2 + side])):
                for j in (0, 2):
                    at = (slab // 2) * 8 + j * 2 + slab % 2
                    right = jnp.concatenate([ref[at], ref[at + 2]], axis=0)
                    term = jnp.dot(lefts[group, j], right, preferred_element_type=F32)
                    total = term if total is None else total + term
            parity = even if slab < 2 else 1 - even
            start = pl.multiple_of((core * 2 + parity) * 512 + (slab % 2) * 256, 256)
            out_ref[:, pl.ds(start, 256)] = total.astype(dtype)


def mix_partner_kernel(x_ref, *refs):
    mix_rows(x_ref, refs[:4], slice(64, 128), refs[4], BF16)


def mix_own_kernel(x_ref, *refs):
    mix_rows(x_ref, refs[:4], slice(0, 64), refs[4], F32)


def sum_kernel(own_ref, other_ref, mixed_ref):
    mixed_ref[...] = (own_ref[...] + other_ref[...].astype(F32)).astype(BF16)


def call(kernel, shapes, n_vmem, scratch=(), flops=0, size=0):
    return pl.pallas_call(
        kernel,
        out_shape=shapes,
        in_specs=[VMEM] * n_vmem,
        out_specs=jax.tree.map(lambda _: VMEM, shapes),
        scratch_shapes=list(scratch),
        compiler_params=pltpu.CompilerParams(vmem_limit_bytes=LIMIT),
        cost_estimate=pl.CostEstimate(flops=flops, bytes_accessed=size, transcendentals=0),
    )


def struct(shape, dtype):
    return jax.ShapeDtypeStruct(shape, dtype)


def join(*parts):
    shape = (sum(p.shape[0] for p in parts),) + parts[0].shape[1:]
    return call(join_kernel, struct(shape, BF16), len(parts), size=1 << 20)(*parts)


def local(tokens, beta, w_query, w_key, w_value, gain, w_out):
    ctx, heads = lax.axis_size("ctx"), lax.axis_size("head")
    rows = tokens.shape[0]
    weights = (w_query, w_key, w_value)

    slab = (DK, 2 * DK)
    a, b = call(pack_kernel, (struct((2,) + slab, BF16),) * 2, 1, size=1 << 19)(tokens)
    a = call(pack_with_w_kernel, struct((4,) + slab, BF16), 2, size=1 << 20)(a, w_out)
    na, nb = swap(a, STREAMS[0][0], ctx, heads), swap(b, STREAMS[1][0], ctx, heads)
    na, nb = lax.optimization_barrier((na, nb))
    a, b = join(a, na), join(b, nb)
    na, nb = swap(a, STREAMS[0][1], ctx, heads), swap(b, STREAMS[1][1], ctx, heads)
    four = struct((4,) + slab, BF16)
    pieces = [None] * 4
    pieces[0], pieces[2], w = call(
        split_kernel, (four, four, struct((8,) + slab, BF16)), 2, size=2 << 20
    )(a, na)
    pieces[1], pieces[3] = call(split_kernel, (four, four), 2, size=1 << 20)(b, nb)
    *_, w = lax.optimization_barrier((*pieces, w))
    other_core = [(c, c ^ 1) for c in range(ctx)]
    w_next = lax.ppermute(w, "ctx", [(c, c ^ 2) for c in range(ctx)])
    arrived = [swap(p, masks[2], ctx, heads) for p, masks in zip(pieces, STREAMS)]
    pieces = [join(p, n) for p, n in zip(pieces, arrived)]
    arrived = [swap(p, masks[3], ctx, heads) for p, masks in zip(pieces, STREAMS)]
    raw = call(
        first_half_kernel, struct((rows, 3 * DK), F32), 7, flops=rows * 1024 * 768, size=5 << 20
    )(*pieces, *weights)
    *arrived, w_next, raw = lax.optimization_barrier((*arrived, w_next, raw))
    w = join(w, w_next)
    far_a = swap(w, (4, 12), ctx, heads)
    w_next = lax.ppermute(w, "ctx", other_core)

    key, wu, states, last, sent = call(
        transition_kernel,
        (
            struct((rows, DK), BF16),
            struct((rows, 2 * DK), BF16),
            struct((rows // CHUNK + 1, DK, 2 * DK), F32),
            struct((DK, 2 * DK), F32),
            struct((DK, 2 * DK), BF16),
        ),
        8,
        scratch=[pltpu.VMEM((rows, 2 * DK), F32)],
        flops=rows * 4096 * 768, size=8 << 20,
    )(raw, *arrived, w_key, w_value, beta.reshape(rows // CHUNK, CHUNK))
    eff_query, partial = call(
        outputs_kernel,
        (struct((rows, DK), BF16), struct((rows, DK), F32)),
        9,
        scratch=[pltpu.VMEM((rows, DK), F32)],
        flops=rows * 2048 * 256, size=4 << 20,
    )(raw, *arrived, w_query, key, wu, states)

    _, w_next = lax.optimization_barrier((sent, w_next))
    far_b = swap(w_next, (4, 12), ctx, heads)
    of_core = lax.ppermute(sent, "ctx", other_core)
    chip = call(
        chip_kernel, struct((DK, 2 * DK), BF16), 2, flops=1 << 23, size=1 << 18
    )(last, of_core)
    of_chip = lax.ppermute(chip, "ctx", [(c, c ^ 2) for c in range(ctx)])
    of_chip, eff_query, partial = lax.optimization_barrier((of_chip, eff_query, partial))
    pair = call(pair_kernel, struct((DK, DK), BF16), 2, flops=1 << 23, size=1 << 18)(chip, of_chip)
    of_pair = lax.ppermute(pair, "ctx", [(c, c ^ 6) for c in range(ctx)])
    normed = call(
        finish_kernel, struct((rows, DK), BF16), 6, flops=rows * 128 * 256, size=2 << 20
    )(of_pair, of_chip, of_core, eff_query, partial, gain[None, :])
    pairs = (((0, 1), (2, 3)), ((0, 3), (1, 2)))
    groups = [
        [c * heads + z * 4 + x for z in pair for x in range(4)]
        for c in range(ctx)
        for pair in pairs[c % 2]
    ]
    spread_rows = lax.all_to_all(
        normed, ("ctx", "head"), 0, 0, tiled=True, axis_index_groups=groups
    ).reshape(8, 2 * rows // heads, DK)

    operands = (spread_rows, w, w_next, far_a, far_b)
    leaving = call(
        mix_partner_kernel, struct((64, 2048), BF16), 5, flops=64 * 2048 * 2048, size=4 << 20
    )(*operands)
    entering = swap(leaving, OPPOSITE, ctx, heads)
    own = call(
        mix_own_kernel, struct((64, 2048), F32), 5, flops=64 * 2048 * 2048, size=4 << 20
    )(*operands)
    return call(sum_kernel, struct((64, 2048), BF16), 2, size=1 << 20)(own, entering)


def solution(mesh):
    placed = (
        P("ctx", "head"),
        P("ctx", "head"),
        P(None, "head"),
        P(None, "head"),
        P(None, "head"),
        P(),
        P("head", None),
    )
    return jax.shard_map(
        local, mesh=mesh, in_specs=placed, out_specs=P(("ctx", "head"), None), check_vma=False
    )
```

```python
import jax
import jax.numpy as jnp
from jax import lax
from jax.experimental import pallas as pl
from jax.experimental.pallas import tpu as pltpu
from jax.sharding import PartitionSpec as P

DK = 128
CHUNK = 128
F32 = jnp.float32
BF16 = jnp.bfloat16
VMEM = pl.BlockSpec(memory_space=pltpu.VMEM)
LIMIT = 14 << 20


def dot(left, right, contract=((1,), (0,))):
    return lax.dot_general(
        left.astype(BF16), right.astype(BF16), (contract, ((), ())), preferred_element_type=F32
    )


def halves(value):
    high = value.astype(BF16)
    return high, (value - high.astype(F32)).astype(BF16)


def dot3(left, right, contract=((1,), (0,))):
    (left_high, left_low), (right_high, right_low) = left, right
    along_left, along_right = contract[0][0], contract[1][0]
    return dot(
        jnp.concatenate([left_high, left_high, left_low], axis=along_left),
        jnp.concatenate([right_high, right_low, right_high], axis=along_right),
        contract,
    )


ALONG_X = ((1, 3), (3, 1))
ALONG_Z = ((4, 12), (12, 4))


OPPOSITE = (12, 4)


def flipped(masks):
    return tuple((odd, even) for even, odd in masks)


OPPOSITE = (12, 4)


def flipped(masks):
    return tuple((odd, even) for even, odd in masks)


STREAMS = (
    ALONG_X + ALONG_Z,
    ALONG_Z + ALONG_X,
    flipped(ALONG_X + ALONG_Z),
    flipped(ALONG_Z + ALONG_X),
)


STREAMS = (
    ALONG_X + ALONG_Z,
    ALONG_Z + ALONG_X,
    ALONG_X + flipped(ALONG_Z),
    ALONG_Z + flipped(ALONG_X),
)


def swap(value, masks, ctx, heads):
    pairs = [
        (c * heads + h, c * heads + (h ^ masks[c % 2])) for c in range(ctx) for h in range(heads)
    ]
    return lax.ppermute(value, ("ctx", "head"), pairs)


def offsets(masks, core):
    order = [0]
    for step in masks:
        order = order + [o ^ step[core] for o in order]
    return order


class Place:
    def __init__(self):
        ctx, head = lax.axis_index("ctx"), lax.axis_index("head")
        self.core, self.y = lax.rem(ctx, 2), lax.div(ctx, 2)
        self.head, self.z, self.x = head, lax.div(head, 4), lax.rem(head, 4)
        self.first_core = self.core == 0

    def by_core(self, first, second):
        return jnp.where(self.first_core, first, second)

    def piece_heads(self, masks):
        return [self.head ^ self.by_core(a, b) for a, b in zip(offsets(masks, 0), offsets(masks, 1))]


def pack_kernel(tokens_ref, a_ref, b_ref):
    for stream, out in enumerate((a_ref, b_ref)):
        for i in range(4):
            start = (2 * stream + i % 2 + 4 * (i // 2)) * DK
            at = (i % 2) * DK
            out[i // 2, :, at : at + DK] = tokens_ref[start : start + DK, :]


def pack_with_w_kernel(piece_ref, w_ref, out_ref):
    place = Place()
    quarter = place.core * 2 + lax.rem(place.y, 2)
    out_ref[:2] = piece_ref[...]
    for k in range(2):
        start = pl.multiple_of(quarter * 512 + k * 256, 256)
        out_ref[2 + k] = w_ref[:, pl.ds(start, 256)]


def join_kernel(*refs):
    out_ref, at = refs[-1], 0
    for ref in refs[:-1]:
        out_ref[at : at + ref.shape[0]] = ref[...]
        at += ref.shape[0]


def split_kernel(one_ref, two_ref, first_ref, second_ref, *w_ref):
    width = one_ref.shape[0] // 2
    for i in range(4):
        source, at = (one_ref, two_ref)[i // 2], width * (i % 2)
        first_ref[i] = source[at]
        second_ref[i] = source[at + 1]
        if w_ref:
            w_ref[0][2 * i : 2 * i + 2] = source[at + 2 : at + 4]


def project_part(heads, pieces_ref, weights):
    total = None
    for p in range(0, 8, 2):
        left = jnp.concatenate(
            [
                jnp.concatenate(
                    [pieces_ref[q, :, i * DK : (i + 1) * DK] for q in (p, p + 1)], axis=1
                )
                for i in range(2)
            ],
            axis=0,
        )
        rows = []
        for q in (p, p + 1):
            start = pl.multiple_of(heads[q] * DK, DK)
            rows.append(jnp.concatenate([w[pl.ds(start, DK), :] for w in weights], axis=1))
        term = jnp.dot(left, jnp.concatenate(rows, axis=0), preferred_element_type=F32)
        total = term if total is None else total + term
    return total


def first_half_kernel(t0, t1, t2, t3, wq, wk, wv, raw_ref):
    place = Place()
    for i, pieces in enumerate((t0, t1, t2, t3)):
        heads = place.piece_heads(STREAMS[i])[:8]
        raw_ref[i * 256 : (i + 1) * 256, :] = project_part(heads, pieces, (wq, wk, wv))


def unit_silu(raw):
    act = raw / (1.0 + jnp.exp(jnp.minimum(-raw, 80.0)))
    return act * lax.rsqrt(jnp.sum(act * act, axis=-1, keepdims=True) + 1e-6)


def transition_kernel(
    raw_ref, t0, t1, t2, t3, wk, wv, beta_ref,
    k_ref, wu_ref, states_ref, last_ref, sent_ref, total_ref,
):
    rows = raw_ref.shape[0]
    count = rows // CHUNK
    place = Place()
    for i, pieces in enumerate((t0, t1, t2, t3)):
        part = slice(i * 256, (i + 1) * 256)
        heads = place.piece_heads(STREAMS[i])[8:]
        total_ref[part, :] = raw_ref[part, DK:] + project_part(heads, pieces, (wk, wv))
    row = lax.broadcasted_iota(jnp.int32, (CHUNK, CHUNK), 0)
    col = lax.broadcasted_iota(jnp.int32, (CHUNK, CHUNK), 1)
    eye = (row == col).astype(F32)

    def below(size):
        return (row // (2 * size) == col // (2 * size)) & (
            (row // size) % 2 == 1
        ) & ((col // size) % 2 == 0)

    keys, rates, lowers, inverses = [], [], [], []
    for b in range(count):
        part = slice(b * CHUNK, (b + 1) * CHUNK)
        key = unit_silu(total_ref[part, :DK])
        key_halves = halves(key)
        k_ref[part, :] = key_halves[0]
        rate = jnp.transpose(jnp.broadcast_to(beta_ref[b : b + 1, :], (CHUNK, CHUNK)))
        gram = dot3(key_halves, key_halves, ((1,), (1,)))
        lower = jnp.where(row > col, rate * gram, 0.0)
        keys.append((key, key_halves))
        rates.append(rate)
        lowers.append(lower)
        inverses.append(eye - jnp.where(below(1), lower, 0.0))
    size = 2
    while size < CHUNK:
        mask = below(size)
        inner = [dot(jnp.where(mask, lo, 0.0), inv) for lo, inv in zip(lowers, inverses)]
        inverses = [inv - dot(inv, x) for inv, x in zip(inverses, inner)]
        size *= 2
    for b in range(count):
        rough = inverses[b].astype(BF16)
        product = dot(
            jnp.concatenate(halves(lowers[b]), axis=1), jnp.concatenate([rough, rough], axis=0)
        )
        residual = eye - rough.astype(F32) - product
        inverses[b] = rough.astype(F32) + dot(rough, residual)
    maps = []
    for b in range(count):
        part = slice(b * CHUNK, (b + 1) * CHUNK)
        value = total_ref[part, DK:]
        both = jnp.concatenate([rates[b] * keys[b][0], rates[b] * value], axis=1)
        wu = dot3(halves(inverses[b]), halves(both))
        wu_ref[part, :] = wu
        maps.append(dot3(keys[b][1], halves(wu), ((0,), (0,))))
    zeros = jnp.zeros((DK, DK), F32)
    half = count // 2
    states = [jnp.concatenate([eye, zeros], axis=1)] * 2
    for b in range(half):
        for side in range(2):
            chunk = side * half + b
            state16 = states[side].astype(BF16)
            states_ref[chunk] = states[side]
            states[side] = (
                states[side]
                - dot(maps[chunk][:, :DK], state16)
                + jnp.concatenate([zeros, maps[chunk][:, DK:]], axis=1)
            )
    states_ref[count] = states[0]
    last = compose(states[1], states[0])
    last_ref[...] = last
    sent_ref[...] = last.astype(BF16)


def outputs_kernel(
    raw_ref, t0, t1, t2, t3, wq, k_ref, wu_ref, states_ref, query_ref, out_ref, total_ref
):
    rows = raw_ref.shape[0]
    count = rows // CHUNK
    place = Place()
    for i, pieces in enumerate((t0, t1, t2, t3)):
        part = slice(i * 256, (i + 1) * 256)
        heads = place.piece_heads(STREAMS[i])[8:]
        total_ref[part, :] = raw_ref[part, :DK] + project_part(heads, pieces, (wq,))
    row = lax.broadcasted_iota(jnp.int32, (CHUNK, CHUNK), 0)
    col = lax.broadcasted_iota(jnp.int32, (CHUNK, CHUNK), 1)
    for b in range(count):
        part = slice(b * CHUNK, (b + 1) * CHUNK)
        query = unit_silu(total_ref[part, :])
        scores = jnp.where(row >= col, dot(query, k_ref[part, :], ((1,), (1,))), 0.0)
        local = dot3(halves(scores), halves(wu_ref[part, :]))
        effective = query - local[:, :DK]
        state = states_ref[b]
        if b >= count // 2:
            state = compose(state, states_ref[count])
        result = dot(effective, state)
        query_ref[part, :] = result[:, :DK].astype(BF16)
        out_ref[part, :] = result[:, DK:] + local[:, DK:]


def compose(later, earlier):
    return dot(later[:, :DK], earlier) + jnp.concatenate(
        [jnp.zeros((DK, DK), F32), later[:, DK:]], axis=1
    )


def apply(step, state):
    return dot(step[:, :DK], state) + step[:, DK:]


def chip_kernel(mine_ref, other_ref, chip_ref):
    mine, other = mine_ref[...], other_ref[...].astype(F32)
    second = Place().core == 1
    chip_ref[...] = compose(
        jnp.where(second, mine, other), jnp.where(second, other, mine)
    ).astype(BF16)


def pair_kernel(mine_ref, other_ref, sent_ref):
    mine, other = mine_ref[...].astype(F32), other_ref[...].astype(F32)
    odd = lax.rem(Place().y, 2) == 1
    sent_ref[...] = apply(jnp.where(odd, mine, other), jnp.where(odd, other, mine)[:, DK:]).astype(
        BF16
    )


def finish_kernel(pair_ref, chip_ref, core_ref, query_ref, out_ref, gain_ref, normed_ref):
    place = Place()
    entering = jnp.where(place.y >= 2, pair_ref[...].astype(F32), 0.0)
    entering = jnp.where(
        lax.rem(place.y, 2) == 1, apply(chip_ref[...].astype(F32), entering), entering
    )
    entering = jnp.where(place.core == 1, apply(core_ref[...].astype(F32), entering), entering)
    recurrent = out_ref[...] + dot(query_ref[...], entering)
    scale = lax.rsqrt(jnp.mean(recurrent * recurrent, axis=-1, keepdims=True) + 1e-5)
    normed = (recurrent * scale * gain_ref[...]).astype(BF16)
    for b in range(16):
        z, x = b // 4, b % 4
        inside = place.by_core(
            lax.div(place.z, 2) == z // 2, (place.z == z) | (place.z == 3 - z)
        )
        seat = place.by_core(jnp.where(inside, z % 2, 1 - z % 2), z // 2)
        slot = (seat * 4 + x) * 2 + jnp.where(inside, 0, 1)
        start = pl.multiple_of(slot * 64, 64)
        normed_ref[pl.ds(start, 64), :] = normed[b * 64 : (b + 1) * 64, :]


def mix_rows(x_ref, refs, rows, out_ref, dtype):
    place = Place()
    seat = place.by_core(lax.rem(place.z, 2), lax.div(place.z, 2))
    along_x = [offsets(ALONG_X, c) for c in range(2)]
    even = lax.rem(place.y, 2)
    for side in range(2):
        core = place.core if side == 0 else 1 - place.core
        order = [
            place.x ^ place.by_core(along_x[side][j], along_x[1 - side][j]) for j in range(4)
        ]
        lefts = {}
        for group in range(2):
            base = (seat if group == 0 else 1 - seat) * 4
            for j in (0, 2):
                lefts[group, j] = jnp.concatenate(
                    [x_ref[base + order[j], rows, :], x_ref[base + order[j + 1], rows, :]], axis=1
                )
        for slab in range(4):
            total = None
            for group, ref in enumerate((refs[side], refs[2 + side])):
                for j in (0, 2):
                    at = (slab // 2) * 8 + j * 2 + slab % 2
                    right = jnp.concatenate([ref[at], ref[at + 2]], axis=0)
                    term = jnp.dot(lefts[group, j], right, preferred_element_type=F32)
                    total = term if total is None else total + term
            parity = even if slab < 2 else 1 - even
            start = pl.multiple_of((core * 2 + parity) * 512 + (slab % 2) * 256, 256)
            out_ref[:, pl.ds(start, 256)] = total.astype(dtype)


def mix_partner_kernel(x_ref, *refs):
    mix_rows(x_ref, refs[:4], slice(64, 128), refs[4], BF16)


def mix_own_kernel(x_ref, *refs):
    mix_rows(x_ref, refs[:4], slice(0, 64), refs[4], F32)


def sum_kernel(own_ref, other_ref, mixed_ref):
    mixed_ref[...] = (own_ref[...] + other_ref[...].astype(F32)).astype(BF16)


def call(kernel, shapes, n_vmem, scratch=(), flops=0, size=0):
    return pl.pallas_call(
        kernel,
        out_shape=shapes,
        in_specs=[VMEM] * n_vmem,
        out_specs=jax.tree.map(lambda _: VMEM, shapes),
        scratch_shapes=list(scratch),
        compiler_params=pltpu.CompilerParams(vmem_limit_bytes=LIMIT),
        cost_estimate=pl.CostEstimate(flops=flops, bytes_accessed=size, transcendentals=0),
    )


def struct(shape, dtype):
    return jax.ShapeDtypeStruct(shape, dtype)


def join(*parts):
    shape = (sum(p.shape[0] for p in parts),) + parts[0].shape[1:]
    return call(join_kernel, struct(shape, BF16), len(parts), size=1 << 20)(*parts)


def local(tokens, beta, w_query, w_key, w_value, gain, w_out):
    ctx, heads = lax.axis_size("ctx"), lax.axis_size("head")
    rows = tokens.shape[0]
    weights = (w_query, w_key, w_value)

    slab = (DK, 2 * DK)
    a, b = call(pack_kernel, (struct((2,) + slab, BF16),) * 2, 1, size=1 << 19)(tokens)
    a = call(pack_with_w_kernel, struct((4,) + slab, BF16), 2, size=1 << 20)(a, w_out)
    na, nb = swap(a, STREAMS[0][0], ctx, heads), swap(b, STREAMS[1][0], ctx, heads)
    na, nb = lax.optimization_barrier((na, nb))
    a, b = join(a, na), join(b, nb)
    na, nb = swap(a, STREAMS[0][1], ctx, heads), swap(b, STREAMS[1][1], ctx, heads)
    four = struct((4,) + slab, BF16)
    pieces = [None] * 4
    pieces[0], pieces[2], w = call(
        split_kernel, (four, four, struct((8,) + slab, BF16)), 2, size=2 << 20
    )(a, na)
    pieces[1], pieces[3] = call(split_kernel, (four, four), 2, size=1 << 20)(b, nb)
    *_, w = lax.optimization_barrier((*pieces, w))
    other_core = [(c, c ^ 1) for c in range(ctx)]
    w_next = lax.ppermute(w, "ctx", [(c, c ^ 2) for c in range(ctx)])
    arrived = [swap(p, masks[2], ctx, heads) for p, masks in zip(pieces, STREAMS)]
    pieces = [join(p, n) for p, n in zip(pieces, arrived)]
    arrived = [swap(p, masks[3], ctx, heads) for p, masks in zip(pieces, STREAMS)]
    raw = call(
        first_half_kernel, struct((rows, 3 * DK), F32), 7, flops=rows * 1024 * 768, size=5 << 20
    )(*pieces, *weights)
    *arrived, w_next, raw = lax.optimization_barrier((*arrived, w_next, raw))
    w = join(w, w_next)
    far_a = swap(w, (4, 12), ctx, heads)
    w_next = lax.ppermute(w, "ctx", other_core)

    key, wu, states, last, sent = call(
        transition_kernel,
        (
            struct((rows, DK), BF16),
            struct((rows, 2 * DK), F32),
            struct((rows // CHUNK + 1, DK, 2 * DK), F32),
            struct((DK, 2 * DK), F32),
            struct((DK, 2 * DK), BF16),
        ),
        8,
        scratch=[pltpu.VMEM((rows, 2 * DK), F32)],
        flops=rows * 4096 * 768, size=8 << 20,
    )(raw, *arrived, w_key, w_value, beta.reshape(rows // CHUNK, CHUNK))
    eff_query, partial = call(
        outputs_kernel,
        (struct((rows, DK), BF16), struct((rows, DK), F32)),
        9,
        scratch=[pltpu.VMEM((rows, DK), F32)],
        flops=rows * 2048 * 256, size=4 << 20,
    )(raw, *arrived, w_query, key, wu, states)

    _, w_next = lax.optimization_barrier((sent, w_next))
    far_b = swap(w_next, (4, 12), ctx, heads)
    of_core = lax.ppermute(sent, "ctx", other_core)
    chip = call(
        chip_kernel, struct((DK, 2 * DK), BF16), 2, flops=1 << 23, size=1 << 18
    )(last, of_core)
    of_chip = lax.ppermute(chip, "ctx", [(c, c ^ 2) for c in range(ctx)])
    of_chip, eff_query, partial = lax.optimization_barrier((of_chip, eff_query, partial))
    pair = call(pair_kernel, struct((DK, DK), BF16), 2, flops=1 << 23, size=1 << 18)(chip, of_chip)
    of_pair = lax.ppermute(pair, "ctx", [(c, c ^ 6) for c in range(ctx)])
    normed = call(
        finish_kernel, struct((rows, DK), BF16), 6, flops=rows * 128 * 256, size=2 << 20
    )(of_pair, of_chip, of_core, eff_query, partial, gain[None, :])
    pairs = (((0, 1), (2, 3)), ((0, 3), (1, 2)))
    groups = [
        [c * heads + z * 4 + x for z in pair for x in range(4)]
        for c in range(ctx)
        for pair in pairs[c % 2]
    ]
    spread_rows = lax.all_to_all(
        normed, ("ctx", "head"), 0, 0, tiled=True, axis_index_groups=groups
    ).reshape(8, 2 * rows // heads, DK)

    operands = (spread_rows, w, w_next, far_a, far_b)
    leaving = call(
        mix_partner_kernel, struct((64, 2048), BF16), 5, flops=64 * 2048 * 2048, size=4 << 20
    )(*operands)
    entering = swap(leaving, OPPOSITE, ctx, heads)
    own = call(
        mix_own_kernel, struct((64, 2048), F32), 5, flops=64 * 2048 * 2048, size=4 << 20
    )(*operands)
    return call(sum_kernel, struct((64, 2048), BF16), 2, size=1 << 20)(own, entering)


def solution(mesh):
    placed = (
        P("ctx", "head"),
        P("ctx", "head"),
        P(None, "head"),
        P(None, "head"),
        P(None, "head"),
        P(),
        P("head", None),
    )
    return jax.shard_map(
        local, mesh=mesh, in_specs=placed, out_specs=P(("ctx", "head"), None), check_vma=False
    )
```

```python
import jax
import jax.numpy as jnp
from jax import lax
from jax.experimental import pallas as pl
from jax.experimental.pallas import tpu as pltpu
from jax.sharding import PartitionSpec as P

DK = 128
CHUNK = 128
F32 = jnp.float32
BF16 = jnp.bfloat16
VMEM = pl.BlockSpec(memory_space=pltpu.VMEM)
LIMIT = 14 << 20


def dot(left, right, contract=((1,), (0,))):
    return lax.dot_general(
        left.astype(BF16), right.astype(BF16), (contract, ((), ())), preferred_element_type=F32
    )


def halves(value):
    high = value.astype(BF16)
    return high, (value - high.astype(F32)).astype(BF16)


def dot3(left, right, contract=((1,), (0,))):
    (left_high, left_low), (right_high, right_low) = left, right
    along_left, along_right = contract[0][0], contract[1][0]
    return dot(
        jnp.concatenate([left_high, left_high, left_low], axis=along_left),
        jnp.concatenate([right_high, right_low, right_high], axis=along_right),
        contract,
    )


ALONG_X = ((1, 3), (3, 1))
ALONG_Z = ((4, 12), (12, 4))


OPPOSITE = (12, 4)


def flipped(masks):
    return tuple((odd, even) for even, odd in masks)


OPPOSITE = (12, 4)


def flipped(masks):
    return tuple((odd, even) for even, odd in masks)


STREAMS = (
    ALONG_X + ALONG_Z,
    ALONG_Z + ALONG_X,
    flipped(ALONG_X + ALONG_Z),
    flipped(ALONG_Z + ALONG_X),
)


STREAMS = (
    ALONG_X + ALONG_Z,
    ALONG_Z + ALONG_X,
    ALONG_X + flipped(ALONG_Z),
    ALONG_Z + flipped(ALONG_X),
)


def swap(value, masks, ctx, heads):
    pairs = [
        (c * heads + h, c * heads + (h ^ masks[c % 2])) for c in range(ctx) for h in range(heads)
    ]
    return lax.ppermute(value, ("ctx", "head"), pairs)


def offsets(masks, core):
    order = [0]
    for step in masks:
        order = order + [o ^ step[core] for o in order]
    return order


class Place:
    def __init__(self):
        ctx, head = lax.axis_index("ctx"), lax.axis_index("head")
        self.core, self.y = lax.rem(ctx, 2), lax.div(ctx, 2)
        self.head, self.z, self.x = head, lax.div(head, 4), lax.rem(head, 4)
        self.first_core = self.core == 0

    def by_core(self, first, second):
        return jnp.where(self.first_core, first, second)

    def piece_heads(self, masks):
        return [self.head ^ self.by_core(a, b) for a, b in zip(offsets(masks, 0), offsets(masks, 1))]


def pack_kernel(tokens_ref, a_ref, b_ref):
    for stream, out in enumerate((a_ref, b_ref)):
        for i in range(4):
            start = (2 * stream + i % 2 + 4 * (i // 2)) * DK
            at = (i % 2) * DK
            out[i // 2, :, at : at + DK] = tokens_ref[start : start + DK, :]


def pack_with_w_kernel(piece_ref, w_ref, out_ref):
    place = Place()
    quarter = place.core * 2 + lax.rem(place.y, 2)
    out_ref[:2] = piece_ref[...]
    for k in range(2):
        start = pl.multiple_of(quarter * 512 + k * 256, 256)
        out_ref[2 + k] = w_ref[:, pl.ds(start, 256)]


def join_kernel(*refs):
    out_ref, at = refs[-1], 0
    for ref in refs[:-1]:
        out_ref[at : at + ref.shape[0]] = ref[...]
        at += ref.shape[0]


def split_kernel(one_ref, two_ref, first_ref, second_ref, *w_ref):
    width = one_ref.shape[0] // 2
    for i in range(4):
        source, at = (one_ref, two_ref)[i // 2], width * (i % 2)
        first_ref[i] = source[at]
        second_ref[i] = source[at + 1]
        if w_ref:
            w_ref[0][2 * i : 2 * i + 2] = source[at + 2 : at + 4]


def project_part(heads, pieces_ref, weights):
    total = None
    for p in range(0, 8, 2):
        left = jnp.concatenate(
            [
                jnp.concatenate(
                    [pieces_ref[q, :, i * DK : (i + 1) * DK] for q in (p, p + 1)], axis=1
                )
                for i in range(2)
            ],
            axis=0,
        )
        rows = []
        for q in (p, p + 1):
            start = pl.multiple_of(heads[q] * DK, DK)
            rows.append(jnp.concatenate([w[pl.ds(start, DK), :] for w in weights], axis=1))
        term = jnp.dot(left, jnp.concatenate(rows, axis=0), preferred_element_type=F32)
        total = term if total is None else total + term
    return total


def first_half_kernel(t0, t1, t2, t3, wq, wk, wv, raw_ref):
    place = Place()
    for i, pieces in enumerate((t0, t1, t2, t3)):
        heads = place.piece_heads(STREAMS[i])[:8]
        raw_ref[i * 256 : (i + 1) * 256, :] = project_part(heads, pieces, (wq, wk, wv))


def unit_silu(raw):
    act = raw / (1.0 + jnp.exp(jnp.minimum(-raw, 80.0)))
    return act * lax.rsqrt(jnp.sum(act * act, axis=-1, keepdims=True) + 1e-6)


def transition_kernel(
    raw_ref, t0, t1, t2, t3, wk, wv, beta_ref,
    k_ref, wu_ref, states_ref, last_ref, sent_ref, total_ref,
):
    rows = raw_ref.shape[0]
    count = rows // CHUNK
    place = Place()
    for i, pieces in enumerate((t0, t1, t2, t3)):
        part = slice(i * 256, (i + 1) * 256)
        heads = place.piece_heads(STREAMS[i])[8:]
        total_ref[part, :] = raw_ref[part, DK:] + project_part(heads, pieces, (wk, wv))
    row = lax.broadcasted_iota(jnp.int32, (CHUNK, CHUNK), 0)
    col = lax.broadcasted_iota(jnp.int32, (CHUNK, CHUNK), 1)
    eye = (row == col).astype(F32)

    def below(size):
        return (row // (2 * size) == col // (2 * size)) & (
            (row // size) % 2 == 1
        ) & ((col // size) % 2 == 0)

    keys, rates, lowers, inverses = [], [], [], []
    for b in range(count):
        part = slice(b * CHUNK, (b + 1) * CHUNK)
        key = unit_silu(total_ref[part, :DK])
        key_halves = halves(key)
        k_ref[part, :] = key_halves[0]
        rate = jnp.transpose(jnp.broadcast_to(beta_ref[b : b + 1, :], (CHUNK, CHUNK)))
        gram = dot3(key_halves, key_halves, ((1,), (1,)))
        lower = jnp.where(row > col, rate * gram, 0.0)
        keys.append((key, key_halves))
        rates.append(rate)
        lowers.append(lower)
        inverses.append(eye - jnp.where(below(1), lower, 0.0))
    size = 2
    while size < CHUNK:
        mask = below(size)
        inner = [dot(jnp.where(mask, lo, 0.0), inv) for lo, inv in zip(lowers, inverses)]
        inverses = [inv - dot(inv, x) for inv, x in zip(inverses, inner)]
        size *= 2
    for b in range(count):
        rough = inverses[b].astype(BF16)
        product = dot(
            jnp.concatenate(halves(lowers[b]), axis=1), jnp.concatenate([rough, rough], axis=0)
        )
        residual = eye - rough.astype(F32) - product
        inverses[b] = rough.astype(F32) + dot(rough, residual)
    maps = []
    for b in range(count):
        part = slice(b * CHUNK, (b + 1) * CHUNK)
        value = total_ref[part, DK:]
        both = jnp.concatenate([rates[b] * keys[b][0], rates[b] * value], axis=1)
        wu = dot3(halves(inverses[b]), halves(both))
        wu_ref[part, :] = wu
        maps.append(dot3(keys[b][1], halves(wu), ((0,), (0,))))
    zeros = jnp.zeros((DK, DK), F32)
    half = count // 2
    states = [jnp.concatenate([eye, zeros], axis=1)] * 2
    for b in range(half):
        for side in range(2):
            chunk = side * half + b
            state16 = states[side].astype(BF16)
            states_ref[chunk] = states[side]
            states[side] = (
                states[side]
                - dot(maps[chunk][:, :DK], state16)
                + jnp.concatenate([zeros, maps[chunk][:, DK:]], axis=1)
            )
    states_ref[count] = states[0]
    last = compose(states[1], states[0])
    last_ref[...] = last
    sent_ref[...] = last.astype(BF16)


def outputs_kernel(
    raw_ref, t0, t1, t2, t3, wq, k_ref, wu_ref, states_ref, query_ref, out_ref, total_ref
):
    rows = raw_ref.shape[0]
    count = rows // CHUNK
    place = Place()
    for i, pieces in enumerate((t0, t1, t2, t3)):
        part = slice(i * 256, (i + 1) * 256)
        heads = place.piece_heads(STREAMS[i])[8:]
        total_ref[part, :] = raw_ref[part, :DK] + project_part(heads, pieces, (wq,))
    row = lax.broadcasted_iota(jnp.int32, (CHUNK, CHUNK), 0)
    col = lax.broadcasted_iota(jnp.int32, (CHUNK, CHUNK), 1)
    for b in range(count):
        part = slice(b * CHUNK, (b + 1) * CHUNK)
        query = unit_silu(total_ref[part, :])
        scores = jnp.where(row >= col, dot(query, k_ref[part, :], ((1,), (1,))), 0.0)
        local = dot3(halves(scores), halves(wu_ref[part, :]))
        effective = query - local[:, :DK]
        state = states_ref[b]
        if b >= count // 2:
            state = compose(state, states_ref[count])
        result = dot(effective, state)
        query_ref[part, :] = result[:, :DK].astype(BF16)
        out_ref[part, :] = result[:, DK:] + local[:, DK:]


def compose(later, earlier):
    return dot(later[:, :DK], earlier) + jnp.concatenate(
        [jnp.zeros((DK, DK), F32), later[:, DK:]], axis=1
    )


def apply(step, state):
    return dot(step[:, :DK], state) + step[:, DK:]


def chip_kernel(mine_ref, other_ref, chip_ref):
    mine, other = mine_ref[...], other_ref[...].astype(F32)
    second = Place().core == 1
    chip_ref[...] = compose(
        jnp.where(second, mine, other), jnp.where(second, other, mine)
    ).astype(BF16)


def pair_kernel(mine_ref, other_ref, sent_ref):
    mine, other = mine_ref[...].astype(F32), other_ref[...].astype(F32)
    odd = lax.rem(Place().y, 2) == 1
    sent_ref[...] = apply(jnp.where(odd, mine, other), jnp.where(odd, other, mine)[:, DK:]).astype(
        BF16
    )


def finish_kernel(pair_ref, chip_ref, core_ref, query_ref, out_ref, gain_ref, normed_ref):
    place = Place()
    entering = jnp.where(place.y >= 2, pair_ref[...].astype(F32), 0.0)
    entering = jnp.where(
        lax.rem(place.y, 2) == 1, apply(chip_ref[...].astype(F32), entering), entering
    )
    entering = jnp.where(place.core == 1, apply(core_ref[...].astype(F32), entering), entering)
    recurrent = out_ref[...] + dot(query_ref[...], entering)
    scale = lax.rsqrt(jnp.mean(recurrent * recurrent, axis=-1, keepdims=True) + 1e-5)
    normed = (recurrent * scale * gain_ref[...]).astype(BF16)
    for b in range(16):
        z, x = b // 4, b % 4
        inside = place.by_core(
            lax.div(place.z, 2) == z // 2, (place.z == z) | (place.z == 3 - z)
        )
        seat = place.by_core(jnp.where(inside, z % 2, 1 - z % 2), z // 2)
        slot = (seat * 4 + x) * 2 + jnp.where(inside, 0, 1)
        start = pl.multiple_of(slot * 64, 64)
        normed_ref[pl.ds(start, 64), :] = normed[b * 64 : (b + 1) * 64, :]


def mix_rows(x_ref, refs, rows, out_ref, dtype, sides=(0, 1)):
    place = Place()
    seat = place.by_core(lax.rem(place.z, 2), lax.div(place.z, 2))
    along_x = [offsets(ALONG_X, c) for c in range(2)]
    even = lax.rem(place.y, 2)
    for side in sides:
        core = place.core if side == 0 else 1 - place.core
        order = [
            place.x ^ place.by_core(along_x[side][j], along_x[1 - side][j]) for j in range(4)
        ]
        lefts = {}
        for group in range(2):
            base = (seat if group == 0 else 1 - seat) * 4
            for j in (0, 2):
                lefts[group, j] = jnp.concatenate(
                    [x_ref[base + order[j], rows, :], x_ref[base + order[j + 1], rows, :]], axis=1
                )
        for slab in range(4):
            total = None
            for group, ref in enumerate((refs[side], refs[2 + side])):
                for j in (0, 2):
                    at = (slab // 2) * 8 + j * 2 + slab % 2
                    right = jnp.concatenate([ref[at], ref[at + 2]], axis=0)
                    term = jnp.dot(lefts[group, j], right, preferred_element_type=F32)
                    total = term if total is None else total + term
            parity = even if slab < 2 else 1 - even
            column = core * 1024 if len(sides) == 2 else 0
            start = pl.multiple_of(column + parity * 512 + (slab % 2) * 256, 256)
            out_ref[:, pl.ds(start, 256)] = total.astype(dtype)


def mix_partner_near_kernel(x_ref, near_ref, far_ref, out_ref):
    mix_rows(x_ref, (near_ref, None, far_ref, None), slice(64, 128), out_ref, BF16, (0,))


def mix_partner_other_kernel(x_ref, near_ref, far_ref, out_ref):
    mix_rows(x_ref, (None, near_ref, None, far_ref), slice(64, 128), out_ref, BF16, (1,))


def mix_own_kernel(x_ref, *refs):
    mix_rows(x_ref, refs[:4], slice(0, 64), refs[4], F32)


def sum_kernel(own_ref, near_ref, other_ref, mixed_ref):
    core = Place().core
    for side, ref in ((core, near_ref), (1 - core, other_ref)):
        columns = pl.ds(pl.multiple_of(side * 1024, 1024), 1024)
        mixed_ref[:, columns] = (own_ref[:, columns] + ref[...].astype(F32)).astype(BF16)


def call(kernel, shapes, n_vmem, scratch=(), flops=0, size=0):
    return pl.pallas_call(
        kernel,
        out_shape=shapes,
        in_specs=[VMEM] * n_vmem,
        out_specs=jax.tree.map(lambda _: VMEM, shapes),
        scratch_shapes=list(scratch),
        compiler_params=pltpu.CompilerParams(vmem_limit_bytes=LIMIT),
        cost_estimate=pl.CostEstimate(flops=flops, bytes_accessed=size, transcendentals=0),
    )


def struct(shape, dtype):
    return jax.ShapeDtypeStruct(shape, dtype)


def join(*parts):
    shape = (sum(p.shape[0] for p in parts),) + parts[0].shape[1:]
    return call(join_kernel, struct(shape, BF16), len(parts), size=1 << 20)(*parts)


def local(tokens, beta, w_query, w_key, w_value, gain, w_out):
    ctx, heads = lax.axis_size("ctx"), lax.axis_size("head")
    rows = tokens.shape[0]
    weights = (w_query, w_key, w_value)

    slab = (DK, 2 * DK)
    a, b = call(pack_kernel, (struct((2,) + slab, BF16),) * 2, 1, size=1 << 19)(tokens)
    a = call(pack_with_w_kernel, struct((4,) + slab, BF16), 2, size=1 << 20)(a, w_out)
    na, nb = swap(a, STREAMS[0][0], ctx, heads), swap(b, STREAMS[1][0], ctx, heads)
    na, nb = lax.optimization_barrier((na, nb))
    a, b = join(a, na), join(b, nb)
    na, nb = swap(a, STREAMS[0][1], ctx, heads), swap(b, STREAMS[1][1], ctx, heads)
    four = struct((4,) + slab, BF16)
    pieces = [None] * 4
    pieces[0], pieces[2], w = call(
        split_kernel, (four, four, struct((8,) + slab, BF16)), 2, size=2 << 20
    )(a, na)
    pieces[1], pieces[3] = call(split_kernel, (four, four), 2, size=1 << 20)(b, nb)
    *_, w = lax.optimization_barrier((*pieces, w))
    other_core = [(c, c ^ 1) for c in range(ctx)]
    w_next = lax.ppermute(w, "ctx", [(c, c ^ 2) for c in range(ctx)])
    arrived = [swap(p, masks[2], ctx, heads) for p, masks in zip(pieces, STREAMS)]
    pieces = [join(p, n) for p, n in zip(pieces, arrived)]
    arrived = [swap(p, masks[3], ctx, heads) for p, masks in zip(pieces, STREAMS)]
    raw = call(
        first_half_kernel, struct((rows, 3 * DK), F32), 7, flops=rows * 1024 * 768, size=5 << 20
    )(*pieces, *weights)
    *arrived, w_next, raw = lax.optimization_barrier((*arrived, w_next, raw))
    w = join(w, w_next)
    far_a = swap(w, (4, 12), ctx, heads)
    w_next = lax.ppermute(w, "ctx", other_core)

    key, wu, states, last, sent = call(
        transition_kernel,
        (
            struct((rows, DK), BF16),
            struct((rows, 2 * DK), F32),
            struct((rows // CHUNK + 1, DK, 2 * DK), F32),
            struct((DK, 2 * DK), F32),
            struct((DK, 2 * DK), BF16),
        ),
        8,
        scratch=[pltpu.VMEM((rows, 2 * DK), F32)],
        flops=rows * 4096 * 768, size=8 << 20,
    )(raw, *arrived, w_key, w_value, beta.reshape(rows // CHUNK, CHUNK))
    eff_query, partial = call(
        outputs_kernel,
        (struct((rows, DK), BF16), struct((rows, DK), F32)),
        9,
        scratch=[pltpu.VMEM((rows, DK), F32)],
        flops=rows * 2048 * 256, size=4 << 20,
    )(raw, *arrived, w_query, key, wu, states)

    _, w_next = lax.optimization_barrier((sent, w_next))
    far_b = swap(w_next, (4, 12), ctx, heads)
    of_core = lax.ppermute(sent, "ctx", other_core)
    chip = call(
        chip_kernel, struct((DK, 2 * DK), BF16), 2, flops=1 << 23, size=1 << 18
    )(last, of_core)
    of_chip = lax.ppermute(chip, "ctx", [(c, c ^ 2) for c in range(ctx)])
    of_chip, eff_query, partial = lax.optimization_barrier((of_chip, eff_query, partial))
    pair = call(pair_kernel, struct((DK, DK), BF16), 2, flops=1 << 23, size=1 << 18)(chip, of_chip)
    of_pair = lax.ppermute(pair, "ctx", [(c, c ^ 6) for c in range(ctx)])
    normed = call(
        finish_kernel, struct((rows, DK), BF16), 6, flops=rows * 128 * 256, size=2 << 20
    )(of_pair, of_chip, of_core, eff_query, partial, gain[None, :])
    pairs = (((0, 1), (2, 3)), ((0, 3), (1, 2)))
    groups = [
        [c * heads + z * 4 + x for z in pair for x in range(4)]
        for c in range(ctx)
        for pair in pairs[c % 2]
    ]
    spread_rows = lax.all_to_all(
        normed, ("ctx", "head"), 0, 0, tiled=True, axis_index_groups=groups
    ).reshape(8, 2 * rows // heads, DK)

    operands = (spread_rows, w, w_next, far_a, far_b)
    half = struct((64, 1024), BF16)
    near = call(mix_partner_near_kernel, half, 3, flops=64 * 2048 * 1024, size=2 << 20)(
        spread_rows, w, far_a
    )
    near = swap(near, OPPOSITE, ctx, heads)
    other = call(mix_partner_other_kernel, half, 3, flops=64 * 2048 * 1024, size=2 << 20)(
        spread_rows, w_next, far_b
    )
    other = swap(other, OPPOSITE, ctx, heads)
    own = call(
        mix_own_kernel, struct((64, 2048), F32), 5, flops=64 * 2048 * 2048, size=4 << 20
    )(*operands)
    return call(sum_kernel, struct((64, 2048), BF16), 3, size=1 << 20)(own, near, other)


def solution(mesh):
    placed = (
        P("ctx", "head"),
        P("ctx", "head"),
        P(None, "head"),
        P(None, "head"),
        P(None, "head"),
        P(),
        P("head", None),
    )
    return jax.shard_map(
        local, mesh=mesh, in_specs=placed, out_specs=P(("ctx", "head"), None), check_vma=False
    )
```
